256 devices in a mesh: row: 32 (over y, z), col: 8 (over x, core).
Axes of the slice: x: 4, y: 4, z: 8, core: 2. Of those that a mesh axis runs over, the one named last changes fastest.
Arguments:
- tensor: float32 [32, 128, 256, 256], P(None, 'row', 'col'), may hold values from -21 to 21
- factor_y: float32 [256, 128], replicated, may hold values from -0.375 to 0.375
- factor_z: float32 [256, 128], replicated, may hold values from -0.375 to 0.375
- factor_s: float32 [32, 16], replicated, may hold values from -1 to 1
Outputs:
- core: float32 [16, 128, 128, 128], P(None, 'row', 'col')
- gram: float32 [128, 128], replicated
The draws below stay inside these ranges and needn't reach their ends.
All inputs are finite; a program needn't handle non-finite values.
Results may differ from the reference program's by a relative error of at most 0.000086.
Values sent between devices are 32-bit elements; how exact they have to be, the bound alone decides.
A program may use at most 64 MiB of HBM per device.

```python
import jax
import jax.numpy as jnp
from jax import lax

SPEC = 32
NZ = 256
RY = 128
RZ = 128
RS = 16
NX = 128
NY = 256


def draw_tensor(key, part):
    key = jax.random.fold_in(key, 11)
    noise_key, scale_key = jax.random.split(key)
    shape = (SPEC, NX + 1, NY, NZ)
    noise = jax.random.truncated_normal(noise_key, -4.0, 4.0, shape, jnp.float32)
    low_end, high_end = (0.3, 3.0)
    mixed = noise[:, 1:] + 0.7 * noise[:, :-1]
    logs = jax.random.uniform(scale_key, (NX,), jnp.float32, jnp.log(low_end), jnp.log(high_end))
    return (mixed * jnp.exp(logs)[None, :, None, None]).astype(jnp.float32)


def scatter_about(rng, dims, deviation, bound, held_as=jnp.bfloat16):
    return jnp.clip(deviation * jax.random.normal(rng, dims, jnp.float32), -bound, bound).astype(held_as)


def setup_inputs(seed: int = 0) -> dict:
    key_list = jax.random.split(jax.random.key(seed), 5)
    return {
        "tensor": draw_tensor(jax.random.fold_in(key_list[4], 71), 0),
        "factor_y": scatter_about(key_list[1], (NY, RY), NY ** -0.5, 0.375, jnp.float32),
        "factor_z": scatter_about(key_list[2], (NZ, RZ), NZ ** -0.5, 0.375, jnp.float32),
        "factor_s": scatter_about(key_list[3], (SPEC, RS), SPEC ** -0.5, 1.0, jnp.float32),
    }


def reference(tensor, factor_y, factor_z, factor_s):
    highest = lax.Precision.HIGHEST
    reduced = jnp.einsum('sxyz,zc->sxyc', tensor, factor_z, precision=highest)
    reduced = jnp.einsum('sxyc,sr->rxyc', reduced, factor_s, precision=highest)
    core = jnp.einsum('rxyc,yb->rxbc', reduced, factor_y, precision=highest)
    gram = jnp.einsum('rxbc,rwbc->xw', core, core, precision=highest) / jnp.float32(RY * RZ * RS)
    return core, gram
```

```python
import functools

import jax
import jax.numpy as jnp
from jax import lax
from jax.experimental import pallas as pl
from jax.experimental.pallas import tpu as pltpu
from jax.sharding import PartitionSpec as P

MESH = pl.DeviceIdType.MESH
F32 = jnp.float32
BF16 = jnp.bfloat16

SX, SY, SZ = 4, 4, 8
COLS, ROWS = 2 * SX, SY * SZ
S, NX, NY, NZ = 32, 4, 32, 256
R, B, C = 16, 128, 128
RL = R // COLS
BL = B // COLS
SCALE = 1.0 / (R * B * C)


def split(a):
    hi = a.astype(BF16)
    lo = (a - hi.astype(F32)).astype(BF16)
    return hi, lo


def dot(a, b):
    return jnp.dot(a, b, preferred_element_type=F32)


def dot_t(a, b):
    return lax.dot_general(a, b, (((1,), (1,)), ((), ())), preferred_element_type=F32)


def add_mod(a, d, n):
    return lax.rem(a + d, n)


def kernel(
    tensor, fy, fz, fs, core_out, gram_out,
    tbuf, send_r, recv_r, core, rows, part, buf_a, buf_b, fz_w, fy_w, fs_w,
    t_sem, s1, r1, s2, r2, so, ro, own_sem, s3, r3, s4, r4, s5, r5,
):
    i = lax.axis_index("row")
    j = lax.axis_index("col")
    y, z = i // SZ, lax.rem(i, SZ)
    x, k = j // 2, lax.rem(j, 2)

    def col_partner(d):
        return add_mod(j, d, COLS)

    def row_partner(d):
        return add_mod(i, d, ROWS)

    def zk_partner(d):
        zz, kk = add_mod(z, d // 2, SZ), add_mod(k, d % 2, 2)
        return zz, kk

    def xy_partner(d):
        return add_mod(x, d // SY, SX), add_mod(y, d % SY, SY)

    loads = [
        pltpu.make_async_copy(tensor.at[:, n], tbuf.at[n], t_sem.at[n]) for n in range(NX)
    ]
    for c in loads:
        c.start()

    barrier = pltpu.get_barrier_semaphore()

    def greet_row(d, _):
        pl.semaphore_signal(barrier, inc=1, device_id=(row_partner(d), j), device_id_type=MESH)
        return 0

    lax.fori_loop(1, ROWS, greet_row, 0)
    for d in range(1, COLS):
        pl.semaphore_signal(barrier, inc=1, device_id=(i, col_partner(d)), device_id_type=MESH)

    zh, zl = split(fz[...])
    fz_w[:, :C] = zh
    fz_w[:, C:] = zl
    yh, yl = split(fy[...].T)
    fy_w[:B] = yh
    fy_w[B:] = yl
    sh, sl = split(fs[...])
    pick_r = (
        lax.broadcasted_iota(jnp.int32, (R * 8, R), 0) // 8
        == lax.broadcasted_iota(jnp.int32, (R * 8, R), 1)
    ).astype(F32).astype(BF16)
    pick_s = (
        lax.broadcasted_iota(jnp.int32, (S, S * 8), 1) // 8
        == lax.broadcasted_iota(jnp.int32, (S, S * 8), 0)
    ).astype(F32).astype(BF16)
    same = (
        lax.broadcasted_iota(jnp.int32, (R * 8, S * 8), 0) % 8
        == lax.broadcasted_iota(jnp.int32, (R * 8, S * 8), 1) % 8
    )
    for part_s, at in ((sh, 0), (sl, R * 8)):
        wide = dot(dot_t(pick_r, part_s).astype(BF16), pick_s)
        fs_w[at : at + R * 8] = jnp.where(same, wide, 0.0).astype(BF16)

    for n in range(NX):
        loads[n].wait()
        for h in range(2):
            t = tbuf[n, :, 16 * h : 16 * h + 16, :].reshape(S * 16, NZ)
            th, tl = split(t)
            u = dot(th, fz_w[...])
            u = u[:, :C] + (u[:, C:] + dot(tl, fz_w[:, :C]))
            u = u.reshape(S, 2, 8, C)
            w = jnp.concatenate([u[:, 0].reshape(S * 8, C), u[:, 1].reshape(S * 8, C)], axis=1)
            wh, wl = split(w)
            v = dot(fs_w[...], wh)
            v = v[: R * 8] + (v[R * 8 :] + dot(fs_w[: R * 8], wl))
            for g in range(2):
                send_r[n, :, 16 * h + 8 * g : 16 * h + 8 * g + 8, :] = v[
                    :, g * C : (g + 1) * C
                ].reshape(R, 8, C)

    pl.semaphore_wait(barrier, ROWS - 1 + COLS - 1)

    mine_y = pl.ds(pl.multiple_of(j * NY, NY), NY)
    for n in range(NX):
        for d in range(1, COLS):
            q = col_partner(d)
            pltpu.make_async_remote_copy(
                src_ref=send_r.at[n, pl.ds(q * RL, RL)],
                dst_ref=recv_r.at[n, :, mine_y, :],
                send_sem=s1,
                recv_sem=r1.at[n],
                device_id=(i, q),
                device_id_type=MESH,
            ).start()
    for n in range(NX):
        recv_r[n, :, mine_y, :] = send_r[n, pl.ds(j * RL, RL)]

    for n in range(NX):
        got = recv_r.at[n, :, pl.ds(0, NY * (COLS - 1)), :]
        pltpu.make_async_copy(got, got, r1.at[n]).wait()
        m = jnp.concatenate([recv_r[n, 0], recv_r[n, 1]], axis=1)
        mh, ml = split(m)
        v = dot(fy_w[...], mh)
        v = v[:B] + (v[B:] + dot(fy_w[:B], ml))
        core[0, n] = v[:, :C]
        core[1, n] = v[:, C:]

        def send_rows(d, _, n=n):
            p = row_partner(d)
            pltpu.make_async_remote_copy(
                src_ref=core.at[p // 16, n, pl.ds(pl.multiple_of(lax.rem(p, 16) * 8, 8), 8), :],
                dst_ref=rows.at[i * NX + n],
                send_sem=s2,
                recv_sem=r2,
                device_id=(p, j),
                device_id_type=MESH,
            ).start()
            return 0

        lax.fori_loop(1, ROWS, send_rows, 0)
        rows[i * NX + n] = core[i // 16, n, pl.ds(pl.multiple_of(lax.rem(i, 16) * 8, 8), 8), :]

    for d in range(1, COLS):
        q = col_partner(d)
        pltpu.make_async_remote_copy(
            src_ref=core.at[:, :, pl.ds(pl.multiple_of(q * BL, BL), BL), :],
            dst_ref=core_out.at[pl.ds(j * RL, RL)],
            send_sem=so,
            recv_sem=ro,
            device_id=(i, q),
            device_id_type=MESH,
        ).start()
    own = pltpu.make_async_copy(
        core.at[:, :, pl.ds(pl.multiple_of(j * BL, BL), BL), :],
        core_out.at[pl.ds(j * RL, RL)],
        own_sem,
    )
    own.start()

    got = rows.at[pl.ds(0, (ROWS - 1) * NX)]
    pltpu.make_async_copy(got, got, r2).wait()
    gh, gl = [], []
    for e in range(8):
        h, l = split(rows[:, e, :])
        gh.append(h)
        gl.append(l)
    gh = jnp.concatenate(gh, axis=1)
    gl = jnp.concatenate(gl, axis=1)
    cross = dot_t(gh, gl)
    part[...] = (dot_t(gh, gh) + (cross + cross.T)).reshape(16, 8, 128)

    mine = z * 2 + k
    for d in range(1, 16):
        zz, kk = zk_partner(d)
        pltpu.make_async_remote_copy(
            src_ref=part.at[zz * 2 + kk],
            dst_ref=buf_a.at[mine],
            send_sem=s3,
            recv_sem=r3,
            device_id=(y * SZ + zz, x * 2 + kk),
            device_id_type=MESH,
        ).start()
    buf_a[mine] = part[mine]
    pltpu.make_async_copy(buf_a.at[pl.ds(0, 15)], buf_a.at[pl.ds(0, 15)], r3).wait()
    total = jnp.sum(buf_a[...], axis=0)

    at_xy = x * SY + y
    buf_b[at_xy] = total
    for d in range(1, 16):
        xx, yy = xy_partner(d)
        pltpu.make_async_remote_copy(
            src_ref=buf_b.at[at_xy],
            dst_ref=buf_b.at[at_xy],
            send_sem=s4,
            recv_sem=r4,
            device_id=(yy * SZ + z, xx * 2 + k),
            device_id_type=MESH,
        ).start()
    pltpu.make_async_copy(buf_b.at[pl.ds(0, 15)], buf_b.at[pl.ds(0, 15)], r4).wait()
    gram_out[mine] = jnp.sum(buf_b[...], axis=0) * SCALE

    for d in range(1, 16):
        zz, kk = zk_partner(d)
        pltpu.make_async_remote_copy(
            src_ref=gram_out.at[mine],
            dst_ref=gram_out.at[mine],
            send_sem=s5,
            recv_sem=r5,
            device_id=(y * SZ + zz, x * 2 + kk),
            device_id_type=MESH,
        ).start()

    sent = send_r.at[:, pl.ds(0, R - RL)]
    pltpu.make_async_copy(sent, sent, s1).wait()
    sent = rows.at[pl.ds(0, (ROWS - 1) * NX)]
    pltpu.make_async_copy(sent, sent, s2).wait()
    sent = core.at[:, :, pl.ds(0, B - BL), :]
    pltpu.make_async_copy(sent, sent, so).wait()
    own.wait()
    for sem in (s3, s4, s5):
        pltpu.make_async_copy(buf_a.at[pl.ds(0, 15)], buf_a.at[pl.ds(0, 15)], sem).wait()
    got = core_out.at[pl.ds(0, R - RL)]
    pltpu.make_async_copy(got, got, ro).wait()
    pltpu.make_async_copy(gram_out.at[pl.ds(0, 15)], gram_out.at[pl.ds(0, 15)], r5).wait()


def body(tensor, factor_y, factor_z, factor_s):
    dma = pltpu.SemaphoreType.DMA
    core, gram = pl.pallas_call(
        kernel,
        out_shape=(
            jax.ShapeDtypeStruct((R, NX, BL, C), F32),
            jax.ShapeDtypeStruct((16, 8, 128), F32),
        ),
        in_specs=[pl.BlockSpec(memory_space=pl.ANY)] + [pl.BlockSpec(memory_space=pltpu.VMEM)] * 3,
        out_specs=(pl.BlockSpec(memory_space=pl.ANY), pl.BlockSpec(memory_space=pltpu.VMEM)),
        scratch_shapes=[
            pltpu.VMEM((NX, S, NY, NZ), F32),
            pltpu.VMEM((NX, R, NY, C), F32),
            pltpu.VMEM((NX, RL, NY * COLS, C), F32),
            pltpu.VMEM((RL, NX, B, C), F32),
            pltpu.VMEM((ROWS * NX, 8, C), F32),
            pltpu.VMEM((16, 8, 128), F32),
            pltpu.VMEM((16, 8, 128), F32),
            pltpu.VMEM((16, 8, 128), F32),
            pltpu.VMEM((NZ, 2 * C), BF16),
            pltpu.VMEM((2 * B, NY * COLS), BF16),
            pltpu.VMEM((2 * R * 8, S * 8), BF16),
            dma((NX,)),
            dma, dma((NX,)),
            dma, dma,
            dma, dma, dma,
            dma, dma,
            dma, dma,
            dma, dma,
        ],
        compiler_params=pltpu.CompilerParams(
            collective_id=0, has_side_effects=True, vmem_limit_bytes=48 * 1024 * 1024
        ),
    )(tensor, factor_y, factor_z, factor_s)
    return core, gram.reshape(128, 128)


def solution(mesh):
    in_specs = (P(None, "row", "col", None), P(), P(), P())
    out_specs = (P(None, "row", "col", None), P())
    return jax.shard_map(body, mesh=mesh, in_specs=in_specs, out_specs=out_specs, check_vma=False)
```

```python
import functools

import jax
import jax.numpy as jnp
from jax import lax
from jax.experimental import pallas as pl
from jax.experimental.pallas import tpu as pltpu
from jax.sharding import PartitionSpec as P

MESH = pl.DeviceIdType.MESH
F32 = jnp.float32
BF16 = jnp.bfloat16

SX, SY, SZ = 4, 4, 8
COLS, ROWS = 2 * SX, SY * SZ
S, NX, NY, NZ = 32, 4, 32, 256
R, B, C = 16, 128, 128
RL = R // COLS
BL = B // COLS
SCALE = 1.0 / (R * B * C)
VMEM_BYTES = 63 * 1024 * 1024


def split(a):
    hi = a.astype(BF16)
    lo = (a - hi.astype(F32)).astype(BF16)
    return hi, lo


def dot(a, b):
    return jnp.dot(a, b, preferred_element_type=F32)


def dot_t(a, b):
    return lax.dot_general(a, b, (((1,), (1,)), ((), ())), preferred_element_type=F32)


def add_mod(a, d, n):
    return lax.rem(a + d, n)


def kernel(
    tensor, fy_hbm, fz_hbm, fs_hbm, core_out, gram_out,
    fy, fz, fs, tbuf, send_r, recv_r, core, rows, part, buf_a, buf_b, fz_w, fy_w, fs_w,
    f_sem, t_sem, s1, r1, s2, r2, so, ro, own_sem, s3, r3, s4, r4, s5, r5,
):
    i = lax.axis_index("row")
    j = lax.axis_index("col")
    y, z = i // SZ, lax.rem(i, SZ)
    x, k = j // 2, lax.rem(j, 2)

    def col_partner(d):
        return add_mod(j, d, COLS)

    def row_partner(d):
        return add_mod(i, d, ROWS)

    def zk_partner(d):
        zz, kk = add_mod(z, d // 2, SZ), add_mod(k, d % 2, 2)
        return zz, kk

    def xy_partner(d):
        return add_mod(x, d // SY, SX), add_mod(y, d % SY, SY)

    loads = [
        pltpu.make_async_copy(tensor.at[:, n], tbuf.at[n], t_sem.at[n]) for n in range(NX)
    ]
    factors = [
        pltpu.make_async_copy(a, b, f_sem.at[n])
        for n, (a, b) in enumerate(((fz_hbm, fz), (fs_hbm, fs), (fy_hbm, fy)))
    ]
    for c in factors[:2] + loads[:1] + factors[2:] + loads[1:]:
        c.start()

    barrier = pltpu.get_barrier_semaphore()

    def greet_row(d, _):
        pl.semaphore_signal(barrier, inc=1, device_id=(row_partner(d), j), device_id_type=MESH)
        return 0

    lax.fori_loop(1, ROWS, greet_row, 0)
    for d in range(1, COLS):
        pl.semaphore_signal(barrier, inc=1, device_id=(i, col_partner(d)), device_id_type=MESH)

    for c in factors:
        c.wait()
    zh, zl = split(fz[...])
    fz_w[:, :C] = zh
    fz_w[:, C:] = zl
    yh, yl = split(fy[...].T)
    fy_w[:B] = yh
    fy_w[B:] = yl
    sh, sl = split(fs[...])
    pick_r = (
        lax.broadcasted_iota(jnp.int32, (R * 8, R), 0) // 8
        == lax.broadcasted_iota(jnp.int32, (R * 8, R), 1)
    ).astype(F32).astype(BF16)
    pick_s = (
        lax.broadcasted_iota(jnp.int32, (S, S * 8), 1) // 8
        == lax.broadcasted_iota(jnp.int32, (S, S * 8), 0)
    ).astype(F32).astype(BF16)
    same = (
        lax.broadcasted_iota(jnp.int32, (R * 8, S * 8), 0) % 8
        == lax.broadcasted_iota(jnp.int32, (R * 8, S * 8), 1) % 8
    )
    for part_s, at in ((sh, 0), (sl, R * 8)):
        wide = dot(dot(pick_r, part_s).astype(BF16), pick_s)
        fs_w[at : at + R * 8] = jnp.where(same, wide, 0.0).astype(BF16)

    for n in range(NX):
        loads[n].wait()
        for h in range(2):
            t = tbuf[n, :, 16 * h : 16 * h + 16, :].reshape(S * 16, NZ)
            th, tl = split(t)
            u = dot(th, fz_w[...])
            u = u[:, :C] + (u[:, C:] + dot(tl, fz_w[:, :C]))
            u = u.reshape(S, 2, 8, C)
            w = jnp.concatenate([u[:, 0].reshape(S * 8, C), u[:, 1].reshape(S * 8, C)], axis=1)
            wh, wl = split(w)
            v = dot(fs_w[...], wh)
            v = v[: R * 8] + (v[R * 8 :] + dot(fs_w[: R * 8], wl))
            for g in range(2):
                send_r[n, :, 16 * h + 8 * g : 16 * h + 8 * g + 8, :] = v[
                    :, g * C : (g + 1) * C
                ].reshape(R, 8, C)

    pl.semaphore_wait(barrier, ROWS - 1 + COLS - 1)

    mine_y = pl.ds(pl.multiple_of(j * NY, NY), NY)
    for n in range(NX):
        for d in range(1, COLS):
            q = col_partner(d)
            pltpu.make_async_remote_copy(
                src_ref=send_r.at[n, pl.ds(q * RL, RL)],
                dst_ref=recv_r.at[n, :, mine_y, :],
                send_sem=s1,
                recv_sem=r1.at[n],
                device_id=(i, q),
                device_id_type=MESH,
            ).start()
    for n in range(NX):
        recv_r[n, :, mine_y, :] = send_r[n, pl.ds(j * RL, RL)]

    for n in range(NX):
        got = recv_r.at[n, :, pl.ds(0, NY * (COLS - 1)), :]
        pltpu.make_async_copy(got, got, r1.at[n]).wait()
        m = jnp.concatenate([recv_r[n, 0], recv_r[n, 1]], axis=1)
        mh, ml = split(m)
        v = dot(fy_w[...], mh)
        v = v[:B] + (v[B:] + dot(fy_w[:B], ml))
        core[0, n] = v[:, :C]
        core[1, n] = v[:, C:]

        def send_rows(d, _, n=n):
            p = row_partner(d)
            pltpu.make_async_remote_copy(
                src_ref=core.at[p // 16, n, pl.ds(pl.multiple_of(lax.rem(p, 16) * 8, 8), 8), :],
                dst_ref=rows.at[i * NX + n],
                send_sem=s2,
                recv_sem=r2,
                device_id=(p, j),
                device_id_type=MESH,
            ).start()
            return 0

        lax.fori_loop(1, ROWS, send_rows, 0)
        rows[i * NX + n] = core[i // 16, n, pl.ds(pl.multiple_of(lax.rem(i, 16) * 8, 8), 8), :]

    for d in range(1, COLS):
        q = col_partner(d)
        pltpu.make_async_remote_copy(
            src_ref=core.at[:, :, pl.ds(pl.multiple_of(q * BL, BL), BL), :],
            dst_ref=core_out.at[pl.ds(j * RL, RL)],
            send_sem=so,
            recv_sem=ro,
            device_id=(i, q),
            device_id_type=MESH,
        ).start()
    own = pltpu.make_async_copy(
        core.at[:, :, pl.ds(pl.multiple_of(j * BL, BL), BL), :],
        core_out.at[pl.ds(j * RL, RL)],
        own_sem,
    )
    own.start()

    got = rows.at[pl.ds(0, (ROWS - 1) * NX)]
    pltpu.make_async_copy(got, got, r2).wait()
    gh, gl = [], []
    for e in range(8):
        h, l = split(rows[:, e, :])
        gh.append(h)
        gl.append(l)
    gh = jnp.concatenate(gh, axis=1)
    gl = jnp.concatenate(gl, axis=1)
    cross = dot_t(gh, gl)
    part[...] = (dot_t(gh, gh) + (cross + cross.T)).reshape(16, 8, 128)

    mine = z * 2 + k
    for d in range(1, 16):
        zz, kk = zk_partner(d)
        pltpu.make_async_remote_copy(
            src_ref=part.at[zz * 2 + kk],
            dst_ref=buf_a.at[mine],
            send_sem=s3,
            recv_sem=r3,
            device_id=(y * SZ + zz, x * 2 + kk),
            device_id_type=MESH,
        ).start()
    buf_a[mine] = part[mine]
    pltpu.make_async_copy(buf_a.at[pl.ds(0, 15)], buf_a.at[pl.ds(0, 15)], r3).wait()
    total = jnp.sum(buf_a[...], axis=0)

    at_xy = x * SY + y
    buf_b[at_xy] = total
    for d in range(1, 16):
        xx, yy = xy_partner(d)
        pltpu.make_async_remote_copy(
            src_ref=buf_b.at[at_xy],
            dst_ref=buf_b.at[at_xy],
            send_sem=s4,
            recv_sem=r4,
            device_id=(yy * SZ + z, xx * 2 + k),
            device_id_type=MESH,
        ).start()
    pltpu.make_async_copy(buf_b.at[pl.ds(0, 15)], buf_b.at[pl.ds(0, 15)], r4).wait()
    gram_out[mine] = jnp.sum(buf_b[...], axis=0) * SCALE

    for d in range(1, 16):
        zz, kk = zk_partner(d)
        pltpu.make_async_remote_copy(
            src_ref=gram_out.at[mine],
            dst_ref=gram_out.at[mine],
            send_sem=s5,
            recv_sem=r5,
            device_id=(y * SZ + zz, x * 2 + kk),
            device_id_type=MESH,
        ).start()

    sent = send_r.at[:, pl.ds(0, R - RL)]
    pltpu.make_async_copy(sent, sent, s1).wait()
    sent = rows.at[pl.ds(0, (ROWS - 1) * NX)]
    pltpu.make_async_copy(sent, sent, s2).wait()
    sent = core.at[:, :, pl.ds(0, B - BL), :]
    pltpu.make_async_copy(sent, sent, so).wait()
    own.wait()
    for sem in (s3, s4, s5):
        pltpu.make_async_copy(buf_a.at[pl.ds(0, 15)], buf_a.at[pl.ds(0, 15)], sem).wait()
    got = core_out.at[pl.ds(0, R - RL)]
    pltpu.make_async_copy(got, got, ro).wait()
    pltpu.make_async_copy(gram_out.at[pl.ds(0, 15)], gram_out.at[pl.ds(0, 15)], r5).wait()


def body(tensor, factor_y, factor_z, factor_s):
    dma = pltpu.SemaphoreType.DMA
    core, gram = pl.pallas_call(
        kernel,
        out_shape=(
            jax.ShapeDtypeStruct((R, NX, BL, C), F32),
            jax.ShapeDtypeStruct((16, 8, 128), F32),
        ),
        in_specs=[pl.BlockSpec(memory_space=pl.ANY)] * 4,
        out_specs=(pl.BlockSpec(memory_space=pl.ANY), pl.BlockSpec(memory_space=pltpu.VMEM)),
        scratch_shapes=[
            pltpu.VMEM((NY * COLS, B), F32),
            pltpu.VMEM((NZ, C), F32),
            pltpu.VMEM((R, S), F32),
            pltpu.VMEM((NX, S, NY, NZ), F32),
            pltpu.VMEM((NX, R, NY, C), F32),
            pltpu.VMEM((NX, RL, NY * COLS, C), F32),
            pltpu.VMEM((RL, NX, B, C), F32),
            pltpu.VMEM((ROWS * NX, 8, C), F32),
            pltpu.VMEM((16, 8, 128), F32),
            pltpu.VMEM((16, 8, 128), F32),
            pltpu.VMEM((16, 8, 128), F32),
            pltpu.VMEM((NZ, 2 * C), BF16),
            pltpu.VMEM((2 * B, NY * COLS), BF16),
            pltpu.VMEM((2 * R * 8, S * 8), BF16),
            dma((3,)),
            dma((NX,)),
            dma, dma((NX,)),
            dma, dma,
            dma, dma, dma,
            dma, dma,
            dma, dma,
            dma, dma,
        ],
        compiler_params=pltpu.CompilerParams(
            collective_id=0, has_side_effects=True, vmem_limit_bytes=VMEM_BYTES
        ),
    )(tensor, factor_y, factor_z, factor_s.T)
    return core, gram.reshape(128, 128)


def solution(mesh):
    in_specs = (P(None, "row", "col", None), P(), P(), P())
    out_specs = (P(None, "row", "col", None), P())
    return jax.shard_map(body, mesh=mesh, in_specs=in_specs, out_specs=out_specs, check_vma=False)
```

```python
import functools

import jax
import jax.numpy as jnp
from jax import lax
from jax.experimental import pallas as pl
from jax.experimental.pallas import tpu as pltpu
from jax.sharding import PartitionSpec as P

MESH = pl.DeviceIdType.MESH
F32 = jnp.float32
BF16 = jnp.bfloat16

SX, SY, SZ = 4, 4, 8
COLS, ROWS = 2 * SX, SY * SZ
S, NX, NY, NZ = 32, 4, 32, 256
R, B, C = 16, 128, 128
RL = R // COLS
BL = B // COLS
SCALE = 1.0 / (R * B * C)
VMEM_BYTES = 63 * 1024 * 1024


def split(a):
    hi = a.astype(BF16)
    lo = (a - hi.astype(F32)).astype(BF16)
    return hi, lo


def dot(a, b):
    return jnp.dot(a, b, preferred_element_type=F32)


def dot_t(a, b):
    return lax.dot_general(a, b, (((1,), (1,)), ((), ())), preferred_element_type=F32)


def add_mod(a, d, n):
    return lax.rem(a + d, n)


def kernel(
    tensor, fy_hbm, fz_hbm, fs_hbm, core_out, gram_out,
    fy, fz, fs, tbuf, send_r, recv_r, core, rows, part, buf_a, buf_b, fz_w, fy_w, fs_w,
    group_in, rows_in, f_sem, t_sem, s1, r1, s2, r2, so, ro, own_sem, s3, r3, s4, r4, s5, r5,
):
    i = lax.axis_index("row")
    j = lax.axis_index("col")
    y, z = i // SZ, lax.rem(i, SZ)
    x, k = j // 2, lax.rem(j, 2)

    def col_partner(d):
        return add_mod(j, d, COLS)

    def row_partner(d):
        return add_mod(i, d, ROWS)

    def zk_partner(d):
        zz, kk = add_mod(z, d // 2, SZ), add_mod(k, d % 2, 2)
        return zz, kk

    def xy_partner(d):
        return add_mod(x, d // SY, SX), add_mod(y, d % SY, SY)

    loads = [
        pltpu.make_async_copy(tensor.at[:, n], tbuf.at[n], t_sem.at[n]) for n in range(NX)
    ]
    factors = [
        pltpu.make_async_copy(a, b, f_sem.at[n])
        for n, (a, b) in enumerate(((fz_hbm, fz), (fs_hbm, fs), (fy_hbm, fy)))
    ]
    for c in factors[:2] + loads[:1] + factors[2:] + loads[1:]:
        c.start()

    barrier = pltpu.get_barrier_semaphore()
    for q in range(COLS):
        if q != 1:

            @pl.when(j != q)
            def _():
                pl.semaphore_signal(barrier, inc=1, device_id=(i, q), device_id_type=MESH)

    for c in factors:
        c.wait()
    zh, zl = split(fz[...])
    fz_w[:, :C] = zh
    fz_w[:, C:] = zl
    yh, yl = split(fy[...].T)
    fy_w[:B] = yh
    fy_w[B:] = yl
    sh, sl = split(fs[...])
    pick_r = (
        lax.broadcasted_iota(jnp.int32, (R * 8, R), 0) // 8
        == lax.broadcasted_iota(jnp.int32, (R * 8, R), 1)
    ).astype(F32).astype(BF16)
    pick_s = (
        lax.broadcasted_iota(jnp.int32, (S, S * 8), 1) // 8
        == lax.broadcasted_iota(jnp.int32, (S, S * 8), 0)
    ).astype(F32).astype(BF16)
    same = (
        lax.broadcasted_iota(jnp.int32, (R * 8, S * 8), 0) % 8
        == lax.broadcasted_iota(jnp.int32, (R * 8, S * 8), 1) % 8
    )
    for part_s, at in ((sh, 0), (sl, R * 8)):
        wide = dot(dot(pick_r, part_s).astype(BF16), pick_s)
        fs_w[at : at + R * 8] = jnp.where(same, wide, 0.0).astype(BF16)

    mine_y = pl.ds(pl.multiple_of(j * NY, NY), NY)
    for n in range(NX):
        loads[n].wait()
        for h in range(2):
            t = tbuf[n, :, 16 * h : 16 * h + 16, :].reshape(S * 16, NZ)
            th, tl = split(t)
            u = dot(th, fz_w[...])
            u = u[:, :C] + (u[:, C:] + dot(tl, fz_w[:, :C]))
            u = u.reshape(S, 2, 8, C)
            w = jnp.concatenate([u[:, 0].reshape(S * 8, C), u[:, 1].reshape(S * 8, C)], axis=1)
            wh, wl = split(w)
            v = dot(fs_w[...], wh)
            v = v[: R * 8] + (v[R * 8 :] + dot(fs_w[: R * 8], wl))
            for g in range(2):
                send_r[n, :, 16 * h + 8 * g : 16 * h + 8 * g + 8, :] = v[
                    :, g * C : (g + 1) * C
                ].reshape(R, 8, C)
        if n == 0:

            @pl.when(j != 1)
            def _():
                pl.semaphore_wait(barrier, COLS - 1)

            @pl.when(j == 0)
            def _():
                pl.semaphore_signal(group_in, inc=1, device_id=(i, 1), device_id_type=MESH)

                def greet_row(d, _):
                    pl.semaphore_signal(
                        barrier, inc=1, device_id=(row_partner(d), 1), device_id_type=MESH
                    )
                    return 0

                lax.fori_loop(1, ROWS, greet_row, 0)

            @pl.when(j == 1)
            def _():
                pl.semaphore_wait(group_in, 1)

        for d in range(1, COLS):
            q = col_partner(d)
            pltpu.make_async_remote_copy(
                src_ref=send_r.at[n, pl.ds(q * RL, RL)],
                dst_ref=recv_r.at[n, :, mine_y, :],
                send_sem=s1,
                recv_sem=r1.at[n],
                device_id=(i, q),
                device_id_type=MESH,
            ).start()

    @pl.when(j == 1)
    def _():
        pl.semaphore_wait(barrier, ROWS - 1)
        for q in range(COLS):
            if q != 1:
                pl.semaphore_signal(rows_in, inc=1, device_id=(i, q), device_id_type=MESH)

    for n in range(NX):
        recv_r[n, :, mine_y, :] = send_r[n, pl.ds(j * RL, RL)]

    for n in range(NX):
        got = recv_r.at[n, :, pl.ds(0, NY * (COLS - 1)), :]
        pltpu.make_async_copy(got, got, r1.at[n]).wait()
        m = jnp.concatenate([recv_r[n, 0], recv_r[n, 1]], axis=1)
        mh, ml = split(m)
        v = dot(fy_w[...], mh)
        v = v[:B] + (v[B:] + dot(fy_w[:B], ml))
        core[0, n] = v[:, :C]
        core[1, n] = v[:, C:]

        if n == 0:

            @pl.when(j != 1)
            def _():
                pl.semaphore_wait(rows_in, 1)

        def send_rows(d, _, n=n):
            p = row_partner(d)
            pltpu.make_async_remote_copy(
                src_ref=core.at[p // 16, n, pl.ds(pl.multiple_of(lax.rem(p, 16) * 8, 8), 8), :],
                dst_ref=rows.at[i * NX + n],
                send_sem=s2,
                recv_sem=r2,
                device_id=(p, j),
                device_id_type=MESH,
            ).start()
            return 0

        lax.fori_loop(1, ROWS, send_rows, 0)
        rows[i * NX + n] = core[i // 16, n, pl.ds(pl.multiple_of(lax.rem(i, 16) * 8, 8), 8), :]

    for d in range(1, COLS):
        q = col_partner(d)
        pltpu.make_async_remote_copy(
            src_ref=core.at[:, :, pl.ds(pl.multiple_of(q * BL, BL), BL), :],
            dst_ref=core_out.at[pl.ds(j * RL, RL)],
            send_sem=so,
            recv_sem=ro,
            device_id=(i, q),
            device_id_type=MESH,
        ).start()
    own = pltpu.make_async_copy(
        core.at[:, :, pl.ds(pl.multiple_of(j * BL, BL), BL), :],
        core_out.at[pl.ds(j * RL, RL)],
        own_sem,
    )
    own.start()

    got = rows.at[pl.ds(0, (ROWS - 1) * NX)]
    pltpu.make_async_copy(got, got, r2).wait()
    gh, gl = [], []
    for e in range(8):
        h, l = split(rows[:, e, :])
        gh.append(h)
        gl.append(l)
    gh = jnp.concatenate(gh, axis=1)
    gl = jnp.concatenate(gl, axis=1)
    cross = dot_t(gh, gl)
    part[...] = (dot_t(gh, gh) + (cross + cross.T)).reshape(16, 8, 128)

    mine = z * 2 + k
    for d in range(1, 16):
        zz, kk = zk_partner(d)
        pltpu.make_async_remote_copy(
            src_ref=part.at[zz * 2 + kk],
            dst_ref=buf_a.at[mine],
            send_sem=s3,
            recv_sem=r3,
            device_id=(y * SZ + zz, x * 2 + kk),
            device_id_type=MESH,
        ).start()
    buf_a[mine] = part[mine]
    pltpu.make_async_copy(buf_a.at[pl.ds(0, 15)], buf_a.at[pl.ds(0, 15)], r3).wait()
    total = jnp.sum(buf_a[...], axis=0)

    at_xy = x * SY + y
    buf_b[at_xy] = total
    for d in range(1, 16):
        xx, yy = xy_partner(d)
        pltpu.make_async_remote_copy(
            src_ref=buf_b.at[at_xy],
            dst_ref=buf_b.at[at_xy],
            send_sem=s4,
            recv_sem=r4,
            device_id=(yy * SZ + z, xx * 2 + k),
            device_id_type=MESH,
        ).start()
    pltpu.make_async_copy(buf_b.at[pl.ds(0, 15)], buf_b.at[pl.ds(0, 15)], r4).wait()
    gram_out[mine] = jnp.sum(buf_b[...], axis=0) * SCALE

    for d in range(1, 16):
        zz, kk = zk_partner(d)
        pltpu.make_async_remote_copy(
            src_ref=gram_out.at[mine],
            dst_ref=gram_out.at[mine],
            send_sem=s5,
            recv_sem=r5,
            device_id=(y * SZ + zz, x * 2 + kk),
            device_id_type=MESH,
        ).start()

    sent = send_r.at[:, pl.ds(0, R - RL)]
    pltpu.make_async_copy(sent, sent, s1).wait()
    sent = rows.at[pl.ds(0, (ROWS - 1) * NX)]
    pltpu.make_async_copy(sent, sent, s2).wait()
    sent = core.at[:, :, pl.ds(0, B - BL), :]
    pltpu.make_async_copy(sent, sent, so).wait()
    own.wait()
    for sem in (s3, s4, s5):
        pltpu.make_async_copy(buf_a.at[pl.ds(0, 15)], buf_a.at[pl.ds(0, 15)], sem).wait()
    got = core_out.at[pl.ds(0, R - RL)]
    pltpu.make_async_copy(got, got, ro).wait()
    pltpu.make_async_copy(gram_out.at[pl.ds(0, 15)], gram_out.at[pl.ds(0, 15)], r5).wait()


def body(tensor, factor_y, factor_z, factor_s):
    dma = pltpu.SemaphoreType.DMA
    core, gram = pl.pallas_call(
        kernel,
        out_shape=(
            jax.ShapeDtypeStruct((R, NX, BL, C), F32),
            jax.ShapeDtypeStruct((16, 8, 128), F32),
        ),
        in_specs=[pl.BlockSpec(memory_space=pl.ANY)] * 4,
        out_specs=(pl.BlockSpec(memory_space=pl.ANY), pl.BlockSpec(memory_space=pltpu.VMEM)),
        scratch_shapes=[
            pltpu.VMEM((NY * COLS, B), F32),
            pltpu.VMEM((NZ, C), F32),
            pltpu.VMEM((R, S), F32),
            pltpu.VMEM((NX, S, NY, NZ), F32),
            pltpu.VMEM((NX, R, NY, C), F32),
            pltpu.VMEM((NX, RL, NY * COLS, C), F32),
            pltpu.VMEM((RL, NX, B, C), F32),
            pltpu.VMEM((ROWS * NX, 8, C), F32),
            pltpu.VMEM((16, 8, 128), F32),
            pltpu.VMEM((16, 8, 128), F32),
            pltpu.VMEM((16, 8, 128), F32),
            pltpu.VMEM((NZ, 2 * C), BF16),
            pltpu.VMEM((2 * B, NY * COLS), BF16),
            pltpu.VMEM((2 * R * 8, S * 8), BF16),
            pltpu.SemaphoreType.REGULAR,
            pltpu.SemaphoreType.REGULAR,
            dma((3,)),
            dma((NX,)),
            dma, dma((NX,)),
            dma, dma,
            dma, dma, dma,
            dma, dma,
            dma, dma,
            dma, dma,
        ],
        compiler_params=pltpu.CompilerParams(
            collective_id=0, has_side_effects=True, vmem_limit_bytes=VMEM_BYTES
        ),
    )(tensor, factor_y, factor_z, factor_s.T)
    return core, gram.reshape(128, 128)


def solution(mesh):
    in_specs = (P(None, "row", "col", None), P(), P(), P())
    out_specs = (P(None, "row", "col", None), P())
    return jax.shard_map(body, mesh=mesh, in_specs=in_specs, out_specs=out_specs, check_vma=False)
```

```python
import functools

import jax
import jax.numpy as jnp
from jax import lax
from jax.experimental import pallas as pl
from jax.experimental.pallas import tpu as pltpu
from jax.sharding import PartitionSpec as P

MESH = pl.DeviceIdType.MESH
F32 = jnp.float32
BF16 = jnp.bfloat16

SX, SY, SZ = 4, 4, 8
COLS, ROWS = 2 * SX, SY * SZ
S, NX, NY, NZ = 32, 4, 32, 256
R, B, C = 16, 128, 128
RL = R // COLS
BL = B // COLS
SCALE = 1.0 / (R * B * C)
FAR_FIRST = (4, 5, 3, 2, 6, 7, 1)
VMEM_BYTES = 63 * 1024 * 1024


def split(a):
    hi = a.astype(BF16)
    lo = (a - hi.astype(F32)).astype(BF16)
    return hi, lo


def dot(a, b):
    return jnp.dot(a, b, preferred_element_type=F32)


def dot_t(a, b):
    return lax.dot_general(a, b, (((1,), (1,)), ((), ())), preferred_element_type=F32)


def add_mod(a, d, n):
    return lax.rem(a + d, n)


def kernel(
    tensor, fy_hbm, fz_hbm, fs_hbm, core_out, gram_out,
    fy, fz, fs, tbuf, send_r, recv_r, core, rows, part, buf_a, buf_b, total, fz_w, fy_w, fs_w,
    mate_in, f_sem, t_sem, s1, r1, s2, r2, so, ro, own_sem, s3, r3, s4, r4, s5, r5,
):
    i = lax.axis_index("row")
    j = lax.axis_index("col")
    y, z = i // SZ, lax.rem(i, SZ)
    x, k = j // 2, lax.rem(j, 2)

    def col_partner(d):
        return add_mod(j, d, COLS)

    def row_partner(d):
        return add_mod(i, d, ROWS)

    loads = [
        pltpu.make_async_copy(tensor.at[:, n], tbuf.at[n], t_sem.at[n]) for n in range(NX)
    ]
    factors = [
        pltpu.make_async_copy(a, b, f_sem.at[n])
        for n, (a, b) in enumerate(((fz_hbm, fz), (fs_hbm, fs), (fy_hbm, fy)))
    ]
    for c in factors[:2] + loads[:1] + factors[2:] + loads[1:]:
        c.start()

    barrier = pltpu.get_barrier_semaphore()

    def greet_col(d, _):
        pl.semaphore_signal(
            barrier, inc=1, device_id=(i, 2 * add_mod(x, d, SX)), device_id_type=MESH
        )
        return 0

    def greet_row(d, _):
        pl.semaphore_signal(
            barrier, inc=1, device_id=(row_partner(d), 2 * x + 1), device_id_type=MESH
        )
        return 0

    for d in range(SX):

        @pl.when(k + d > 0)
        def _():
            greet_col(d, 0)

    lax.fori_loop(1, ROWS, greet_row, 0)

    for c in factors:
        c.wait()
    zh, zl = split(fz[...])
    fz_w[:, :C] = zh
    fz_w[:, C:] = zl
    yh, yl = split(fy[...].T)
    fy_w[:B] = yh
    fy_w[B:] = yl
    sh, sl = split(fs[...])
    pick_r = (
        lax.broadcasted_iota(jnp.int32, (R * 8, R), 0) // 8
        == lax.broadcasted_iota(jnp.int32, (R * 8, R), 1)
    ).astype(F32).astype(BF16)
    pick_s = (
        lax.broadcasted_iota(jnp.int32, (S, S * 8), 1) // 8
        == lax.broadcasted_iota(jnp.int32, (S, S * 8), 0)
    ).astype(F32).astype(BF16)
    same = (
        lax.broadcasted_iota(jnp.int32, (R * 8, S * 8), 0) % 8
        == lax.broadcasted_iota(jnp.int32, (R * 8, S * 8), 1) % 8
    )
    for part_s, at in ((sh, 0), (sl, R * 8)):
        wide = dot(dot(pick_r, part_s).astype(BF16), pick_s)
        fs_w[at : at + R * 8] = jnp.where(same, wide, 0.0).astype(BF16)

    mine_y = pl.ds(pl.multiple_of(j * NY, NY), NY)
    for n in range(NX):
        loads[n].wait()
        for h in range(2):
            t = tbuf[n, :, 16 * h : 16 * h + 16, :].reshape(S * 16, NZ)
            th, tl = split(t)
            u = dot(th, fz_w[...])
            u = u[:, :C] + (u[:, C:] + dot(tl, fz_w[:, :C]))
            u = u.reshape(S, 2, 8, C)
            w = jnp.concatenate([u[:, 0].reshape(S * 8, C), u[:, 1].reshape(S * 8, C)], axis=1)
            wh, wl = split(w)
            v = dot(fs_w[...], wh)
            v = v[: R * 8] + (v[R * 8 :] + dot(fs_w[: R * 8], wl))
            for g in range(2):
                send_r[n, :, 16 * h + 8 * g : 16 * h + 8 * g + 8, :] = v[
                    :, g * C : (g + 1) * C
                ].reshape(R, 8, C)
        if n == 0:

            @pl.when(k == 0)
            def _():
                pl.semaphore_wait(barrier, COLS - 1)
                pl.semaphore_signal(mate_in, inc=1, device_id=(i, j + 1), device_id_type=MESH)

            @pl.when(k == 1)
            def _():
                pl.semaphore_wait(mate_in, 1)

        for rank in range(RL):
            for d in FAR_FIRST:
                q = col_partner(d)
                pltpu.make_async_remote_copy(
                    src_ref=send_r.at[n, q * RL + rank],
                    dst_ref=recv_r.at[n, rank, mine_y, :],
                    send_sem=s1,
                    recv_sem=r1.at[n, rank],
                    device_id=(i, q),
                    device_id_type=MESH,
                ).start()

    @pl.when(k == 1)
    def _():
        pl.semaphore_wait(barrier, 2 * (ROWS - 1))
        pl.semaphore_signal(mate_in, inc=1, device_id=(i, j - 1), device_id_type=MESH)

    for n in range(NX):
        recv_r[n, :, mine_y, :] = send_r[n, pl.ds(j * RL, RL)]

    def block(p):
        return pl.ds(pl.multiple_of(p // RL * 8, 8), 8)

    for n in range(NX):
        for rank in range(RL):
            got = recv_r.at[n, rank, pl.ds(0, NY * (COLS - 1)), :]
            pltpu.make_async_copy(got, got, r1.at[n, rank]).wait()
            mh, ml = split(recv_r[n, rank])
            v = dot(fy_w[...], mh)
            core[rank, n] = v[:B] + (v[B:] + dot(fy_w[:B], ml))
            if n == 0 and rank == 0:

                @pl.when(k == 0)
                def _():
                    pl.semaphore_wait(mate_in, 1)

            def send_rows(d, _, n=n, rank=rank):
                p = lax.rem(i // RL + d, ROWS // RL) * RL + rank

                @pl.when(p != i)
                def _():
                    pltpu.make_async_remote_copy(
                        src_ref=core.at[rank, n, block(p), :],
                        dst_ref=rows.at[i * NX + n],
                        send_sem=s2,
                        recv_sem=r2,
                        device_id=(p, j),
                        device_id_type=MESH,
                    ).start()

                return 0

            lax.fori_loop(0, ROWS // RL, send_rows, 0)
        rows[i * NX + n] = core[lax.rem(i, RL), n, block(i), :]

    for d in range(1, COLS):
        q = col_partner(d)
        pltpu.make_async_remote_copy(
            src_ref=core.at[:, :, pl.ds(pl.multiple_of(q * BL, BL), BL), :],
            dst_ref=core_out.at[pl.ds(j * RL, RL)],
            send_sem=so,
            recv_sem=ro,
            device_id=(i, q),
            device_id_type=MESH,
        ).start()
    own = pltpu.make_async_copy(
        core.at[:, :, pl.ds(pl.multiple_of(j * BL, BL), BL), :],
        core_out.at[pl.ds(j * RL, RL)],
        own_sem.at[0],
    )
    own.start()

    got = rows.at[pl.ds(0, (ROWS - 1) * NX)]
    pltpu.make_async_copy(got, got, r2).wait()
    gh, gl = [], []
    for e in range(8):
        h, l = split(rows[:, e, :])
        gh.append(h)
        gl.append(l)
    gh = jnp.concatenate(gh, axis=1)
    gl = jnp.concatenate(gl, axis=1)
    g = dot_t(jnp.concatenate([gh, gl], axis=0), gh)
    cross = g[128:]
    part[...] = (g[:128] + (cross + cross.T)).reshape(16, 8, 128)

    at_xy, at_zk = x * SY + y, z * 2 + k

    def over_xy(d):
        xx, yy = add_mod(x, d // SY, SX), add_mod(y, d % SY, SY)
        return xx * SY + yy, (yy * SZ + z, xx * 2 + k)

    def over_zk(d):
        zz, kk = add_mod(z, d // 2, SZ), add_mod(k, d % 2, 2)
        return (y * SZ + zz, x * 2 + kk)

    for d in range(1, 16):
        slot, device = over_xy(d)
        pltpu.make_async_remote_copy(
            src_ref=part.at[slot],
            dst_ref=buf_a.at[at_xy],
            send_sem=s3,
            recv_sem=r3,
            device_id=device,
            device_id_type=MESH,
        ).start()
    buf_a[at_xy] = part[at_xy]
    pltpu.make_async_copy(buf_a.at[pl.ds(0, 15)], buf_a.at[pl.ds(0, 15)], r3).wait()

    buf_b[at_zk] = jnp.sum(buf_a[...], axis=0)
    for d in range(1, 16):
        pltpu.make_async_remote_copy(
            src_ref=buf_b.at[at_zk],
            dst_ref=buf_b.at[at_zk],
            send_sem=s4,
            recv_sem=r4,
            device_id=over_zk(d),
            device_id_type=MESH,
        ).start()
    pltpu.make_async_copy(buf_b.at[pl.ds(0, 15)], buf_b.at[pl.ds(0, 15)], r4).wait()
    total[...] = jnp.sum(buf_b[...], axis=0) * SCALE

    for d in range(1, 16):
        pltpu.make_async_remote_copy(
            src_ref=total,
            dst_ref=gram_out.at[at_xy],
            send_sem=s5,
            recv_sem=r5,
            device_id=over_xy(d)[1],
            device_id_type=MESH,
        ).start()
    own_gram = pltpu.make_async_copy(total, gram_out.at[at_xy], own_sem.at[1])
    own_gram.start()

    sent = send_r.at[:, pl.ds(0, R - RL)]
    pltpu.make_async_copy(sent, sent, s1).wait()
    sent = rows.at[pl.ds(0, (ROWS - 1) * NX)]
    pltpu.make_async_copy(sent, sent, s2).wait()
    sent = core.at[:, :, pl.ds(0, B - BL), :]
    pltpu.make_async_copy(sent, sent, so).wait()
    own.wait()
    own_gram.wait()
    for sem in (s3, s4, s5):
        pltpu.make_async_copy(buf_a.at[pl.ds(0, 15)], buf_a.at[pl.ds(0, 15)], sem).wait()
    got = core_out.at[pl.ds(0, R - RL)]
    pltpu.make_async_copy(got, got, ro).wait()
    pltpu.make_async_copy(gram_out.at[pl.ds(0, 15)], gram_out.at[pl.ds(0, 15)], r5).wait()


def body(tensor, factor_y, factor_z, factor_s):
    dma = pltpu.SemaphoreType.DMA
    core, gram = pl.pallas_call(
        kernel,
        out_shape=(
            jax.ShapeDtypeStruct((R, NX, BL, C), F32),
            jax.ShapeDtypeStruct((16, 8, 128), F32),
        ),
        in_specs=[pl.BlockSpec(memory_space=pl.ANY)] * 4,
        out_specs=(pl.BlockSpec(memory_space=pl.ANY), pl.BlockSpec(memory_space=pl.ANY)),
        scratch_shapes=[
            pltpu.VMEM((NY * COLS, B), F32),
            pltpu.VMEM((NZ, C), F32),
            pltpu.VMEM((R, S), F32),
            pltpu.VMEM((NX, S, NY, NZ), F32),
            pltpu.VMEM((NX, R, NY, C), F32),
            pltpu.VMEM((NX, RL, NY * COLS, C), F32),
            pltpu.VMEM((RL, NX, B, C), F32),
            pltpu.VMEM((ROWS * NX, 8, C), F32),
            pltpu.VMEM((16, 8, 128), F32),
            pltpu.VMEM((16, 8, 128), F32),
            pltpu.VMEM((16, 8, 128), F32),
            pltpu.VMEM((8, 128), F32),
            pltpu.VMEM((NZ, 2 * C), BF16),
            pltpu.VMEM((2 * B, NY * COLS), BF16),
            pltpu.VMEM((2 * R * 8, S * 8), BF16),
            pltpu.SemaphoreType.REGULAR,
            dma((3,)),
            dma((NX,)),
            dma, dma((NX, RL)),
            dma, dma,
            dma, dma, dma((2,)),
            dma, dma,
            dma, dma,
            dma, dma,
        ],
        compiler_params=pltpu.CompilerParams(
            collective_id=0, has_side_effects=True, vmem_limit_bytes=VMEM_BYTES
        ),
    )(tensor, factor_y, factor_z, factor_s.T)
    return core, gram.reshape(128, 128)


def solution(mesh):
    in_specs = (P(None, "row", "col", None), P(), P(), P())
    out_specs = (P(None, "row", "col", None), P())
    return jax.shard_map(body, mesh=mesh, in_specs=in_specs, out_specs=out_specs, check_vma=False)
```

```python
import functools

import jax
import jax.numpy as jnp
from jax import lax
from jax.experimental import pallas as pl
from jax.experimental.pallas import tpu as pltpu
from jax.sharding import PartitionSpec as P

MESH = pl.DeviceIdType.MESH
F32 = jnp.float32
BF16 = jnp.bfloat16

SX, SY, SZ = 4, 4, 8
COLS, ROWS = 2 * SX, SY * SZ
S, NX, NY, NZ = 32, 4, 32, 256
R, B, C = 16, 128, 128
RL = R // COLS
BL = B // COLS
SCALE = 1.0 / (R * B * C)
FAR_FIRST = (4, 5, 3, 2, 6, 7, 1)
VMEM_BYTES = 40 * 1024 * 1024


def split(a):
    hi = a.astype(BF16)
    lo = (a - hi.astype(F32)).astype(BF16)
    return hi, lo


def dot(a, b):
    return jnp.dot(a, b, preferred_element_type=F32)


def dot_t(a, b):
    return lax.dot_general(a, b, (((1,), (1,)), ((), ())), preferred_element_type=F32)


def add_mod(a, d, n):
    return lax.rem(a + d, n)


def kernel(
    tensor, fy_hbm, fz_hbm, fs_hbm, core_out, gram_out,
    fy, fz, fs, tbuf, send_r, recv_r, core, rows, part, buf_a, buf_b, total, fz_w, fy_w, fs_w,
    mate_in, f_sem, t_sem, s1, r1, s2, r2, so, ro, own_sem, s3, r3, s4, r4, s5, r5,
):
    i = lax.axis_index("row")
    j = lax.axis_index("col")
    y, z = i // SZ, lax.rem(i, SZ)
    x, k = j // 2, lax.rem(j, 2)

    def col_partner(d):
        return add_mod(j, d, COLS)

    def row_partner(d):
        return add_mod(i, d, ROWS)

    loads = [
        pltpu.make_async_copy(tensor.at[:, n], tbuf.at[n], t_sem.at[n]) for n in range(NX)
    ]
    factors = [
        pltpu.make_async_copy(a, b, f_sem.at[n])
        for n, (a, b) in enumerate(((fz_hbm, fz), (fs_hbm, fs), (fy_hbm, fy)))
    ]
    for c in factors[:2] + loads[:1] + factors[2:] + loads[1:]:
        c.start()

    barrier = pltpu.get_barrier_semaphore()

    def greet_col(d, _):
        pl.semaphore_signal(
            barrier, inc=1, device_id=(i, 2 * add_mod(x, d, SX)), device_id_type=MESH
        )
        return 0

    def greet_row(d, _):
        pl.semaphore_signal(
            barrier, inc=1, device_id=(row_partner(d), 2 * x + 1), device_id_type=MESH
        )
        return 0

    for d in range(SX):

        @pl.when(k + d > 0)
        def _():
            greet_col(d, 0)

    lax.fori_loop(1, ROWS, greet_row, 0)

    for c in factors:
        c.wait()
    zh, zl = split(fz[...])
    fz_w[:, :C] = zh
    fz_w[:, C:] = zl
    yh, yl = split(fy[...].T)
    fy_w[:B] = yh
    fy_w[B:] = yl
    sh, sl = split(fs[...])
    pick_r = (
        lax.broadcasted_iota(jnp.int32, (R * 8, R), 0) // 8
        == lax.broadcasted_iota(jnp.int32, (R * 8, R), 1)
    ).astype(F32).astype(BF16)
    pick_s = (
        lax.broadcasted_iota(jnp.int32, (S, S * 8), 1) // 8
        == lax.broadcasted_iota(jnp.int32, (S, S * 8), 0)
    ).astype(F32).astype(BF16)
    same = (
        lax.broadcasted_iota(jnp.int32, (R * 8, S * 8), 0) % 8
        == lax.broadcasted_iota(jnp.int32, (R * 8, S * 8), 1) % 8
    )
    for part_s, at in ((sh, 0), (sl, R * 8)):
        wide = dot(dot(pick_r, part_s).astype(BF16), pick_s)
        fs_w[at : at + R * 8] = jnp.where(same, wide, 0.0).astype(BF16)

    mine_y = pl.ds(pl.multiple_of(j * NY, NY), NY)
    for n in range(NX):
        loads[n].wait()
        for h in range(2):
            t = tbuf[n, :, 16 * h : 16 * h + 16, :].reshape(S * 16, NZ)
            th, tl = split(t)
            u = dot(th, fz_w[...])
            u = u[:, :C] + (u[:, C:] + dot(tl, fz_w[:, :C]))
            u = u.reshape(S, 2, 8, C)
            w = jnp.concatenate([u[:, 0].reshape(S * 8, C), u[:, 1].reshape(S * 8, C)], axis=1)
            wh, wl = split(w)
            v = dot(fs_w[...], wh)
            v = v[: R * 8] + (v[R * 8 :] + dot(fs_w[: R * 8], wl))
            for g in range(2):
                send_r[n, :, 16 * h + 8 * g : 16 * h + 8 * g + 8, :] = v[
                    :, g * C : (g + 1) * C
                ].reshape(R, 8, C)
        if n == 0:

            @pl.when(k == 0)
            def _():
                pl.semaphore_wait(barrier, COLS - 1)
                pl.semaphore_signal(mate_in, inc=1, device_id=(i, j + 1), device_id_type=MESH)

            @pl.when(k == 1)
            def _():
                pl.semaphore_wait(mate_in, 1)

        for rank in range(RL):
            for d in FAR_FIRST:
                q = col_partner(d)
                pltpu.make_async_remote_copy(
                    src_ref=send_r.at[n, q * RL + rank],
                    dst_ref=recv_r.at[n, rank, mine_y, :],
                    send_sem=s1,
                    recv_sem=r1.at[n, rank],
                    device_id=(i, q),
                    device_id_type=MESH,
                ).start()

    @pl.when(k == 1)
    def _():
        pl.semaphore_wait(barrier, 2 * (ROWS - 1))
        pl.semaphore_signal(mate_in, inc=1, device_id=(i, j - 1), device_id_type=MESH)

    for n in range(NX):
        recv_r[n, :, mine_y, :] = send_r[n, pl.ds(j * RL, RL)]

    def block(p):
        return pl.ds(pl.multiple_of(p // RL * 8, 8), 8)

    for n in range(NX):
        for rank in range(RL):
            got = recv_r.at[n, rank, pl.ds(0, NY * (COLS - 1)), :]
            pltpu.make_async_copy(got, got, r1.at[n, rank]).wait()
            mh, ml = split(recv_r[n, rank])
            v = dot(fy_w[...], mh)
            core[rank, n] = v[:B] + (v[B:] + dot(fy_w[:B], ml))
            if n == 0 and rank == 0:

                @pl.when(k == 0)
                def _():
                    pl.semaphore_wait(mate_in, 1)

            def send_rows(d, _, n=n, rank=rank):
                p = lax.rem(i // RL + d, ROWS // RL) * RL + rank

                @pl.when(p != i)
                def _():
                    pltpu.make_async_remote_copy(
                        src_ref=core.at[rank, n, block(p), :],
                        dst_ref=rows.at[i * NX + n],
                        send_sem=s2,
                        recv_sem=r2,
                        device_id=(p, j),
                        device_id_type=MESH,
                    ).start()

                return 0

            lax.fori_loop(0, ROWS // RL, send_rows, 0)
        rows[i * NX + n] = core[lax.rem(i, RL), n, block(i), :]

    for d in range(1, COLS):
        q = col_partner(d)
        pltpu.make_async_remote_copy(
            src_ref=core.at[:, :, pl.ds(pl.multiple_of(q * BL, BL), BL), :],
            dst_ref=core_out.at[pl.ds(j * RL, RL)],
            send_sem=so,
            recv_sem=ro,
            device_id=(i, q),
            device_id_type=MESH,
        ).start()
    own = pltpu.make_async_copy(
        core.at[:, :, pl.ds(pl.multiple_of(j * BL, BL), BL), :],
        core_out.at[pl.ds(j * RL, RL)],
        own_sem.at[0],
    )
    own.start()

    got = rows.at[pl.ds(0, (ROWS - 1) * NX)]
    pltpu.make_async_copy(got, got, r2).wait()
    gh, gl = [], []
    for e in range(8):
        h, l = split(rows[:, e, :])
        gh.append(h)
        gl.append(l)
    gh = jnp.concatenate(gh, axis=1)
    gl = jnp.concatenate(gl, axis=1)
    g = dot_t(jnp.concatenate([gh, gl], axis=0), gh)
    cross = g[128:]
    part[...] = (g[:128] + (cross + cross.T)).reshape(16, 8, 128)

    at_xy, at_zk = x * SY + y, z * 2 + k

    def over_xy(d):
        xx, yy = add_mod(x, d // SY, SX), add_mod(y, d % SY, SY)
        return xx * SY + yy, (yy * SZ + z, xx * 2 + k)

    def over_zk(d):
        zz, kk = add_mod(z, d // 2, SZ), add_mod(k, d % 2, 2)
        return (y * SZ + zz, x * 2 + kk)

    for d in range(1, 16):
        slot, device = over_xy(d)
        pltpu.make_async_remote_copy(
            src_ref=part.at[slot],
            dst_ref=buf_a.at[at_xy],
            send_sem=s3,
            recv_sem=r3,
            device_id=device,
            device_id_type=MESH,
        ).start()
    buf_a[at_xy] = part[at_xy]
    pltpu.make_async_copy(buf_a.at[pl.ds(0, 15)], buf_a.at[pl.ds(0, 15)], r3).wait()

    buf_b[at_zk] = jnp.sum(buf_a[...], axis=0)
    for d in range(1, 16):
        pltpu.make_async_remote_copy(
            src_ref=buf_b.at[at_zk],
            dst_ref=buf_b.at[at_zk],
            send_sem=s4,
            recv_sem=r4,
            device_id=over_zk(d),
            device_id_type=MESH,
        ).start()
    pltpu.make_async_copy(buf_b.at[pl.ds(0, 15)], buf_b.at[pl.ds(0, 15)], r4).wait()
    total[...] = jnp.sum(buf_b[...], axis=0) * SCALE

    for d in range(1, 16):
        pltpu.make_async_remote_copy(
            src_ref=total,
            dst_ref=gram_out.at[at_xy],
            send_sem=s5,
            recv_sem=r5,
            device_id=over_xy(d)[1],
            device_id_type=MESH,
        ).start()
    own_gram = pltpu.make_async_copy(total, gram_out.at[at_xy], own_sem.at[1])
    own_gram.start()

    sent = send_r.at[:, pl.ds(0, R - RL)]
    pltpu.make_async_copy(sent, sent, s1).wait()
    sent = rows.at[pl.ds(0, (ROWS - 1) * NX)]
    pltpu.make_async_copy(sent, sent, s2).wait()
    sent = core.at[:, :, pl.ds(0, B - BL), :]
    pltpu.make_async_copy(sent, sent, so).wait()
    own.wait()
    own_gram.wait()
    for sem in (s3, s4, s5):
        pltpu.make_async_copy(buf_a.at[pl.ds(0, 15)], buf_a.at[pl.ds(0, 15)], sem).wait()
    got = core_out.at[pl.ds(0, R - RL)]
    pltpu.make_async_copy(got, got, ro).wait()
    pltpu.make_async_copy(gram_out.at[pl.ds(0, 15)], gram_out.at[pl.ds(0, 15)], r5).wait()


def in_hbm(a):
    return pltpu.with_memory_space_constraint(a, pltpu.HBM)


def body(tensor, factor_y, factor_z, factor_s):
    dma = pltpu.SemaphoreType.DMA
    core, gram = pl.pallas_call(
        kernel,
        out_shape=(
            jax.ShapeDtypeStruct((R, NX, BL, C), F32),
            jax.ShapeDtypeStruct((16, 8, 128), F32),
        ),
        in_specs=[pl.BlockSpec(memory_space=pltpu.HBM)] * 4,
        out_specs=(pl.BlockSpec(memory_space=pl.ANY), pl.BlockSpec(memory_space=pl.ANY)),
        scratch_shapes=[
            pltpu.VMEM((NY * COLS, B), F32),
            pltpu.VMEM((NZ, C), F32),
            pltpu.VMEM((R, S), F32),
            pltpu.VMEM((NX, S, NY, NZ), F32),
            pltpu.VMEM((NX, R, NY, C), F32),
            pltpu.VMEM((NX, RL, NY * COLS, C), F32),
            pltpu.VMEM((RL, NX, B, C), F32),
            pltpu.VMEM((ROWS * NX, 8, C), F32),
            pltpu.VMEM((16, 8, 128), F32),
            pltpu.VMEM((16, 8, 128), F32),
            pltpu.VMEM((16, 8, 128), F32),
            pltpu.VMEM((8, 128), F32),
            pltpu.VMEM((NZ, 2 * C), BF16),
            pltpu.VMEM((2 * B, NY * COLS), BF16),
            pltpu.VMEM((2 * R * 8, S * 8), BF16),
            pltpu.SemaphoreType.REGULAR,
            dma((3,)),
            dma((NX,)),
            dma, dma((NX, RL)),
            dma, dma,
            dma, dma, dma((2,)),
            dma, dma,
            dma, dma,
            dma, dma,
        ],
        compiler_params=pltpu.CompilerParams(
            collective_id=0, has_side_effects=True, vmem_limit_bytes=VMEM_BYTES
        ),
    )(*(in_hbm(a) for a in (tensor, factor_y, factor_z, factor_s.T)))
    return core, gram.reshape(128, 128)


def solution(mesh):
    in_specs = (P(None, "row", "col", None), P(), P(), P())
    out_specs = (P(None, "row", "col", None), P())
    return jax.shard_map(body, mesh=mesh, in_specs=in_specs, out_specs=out_specs, check_vma=False)
```

```python
import functools

import jax
import jax.numpy as jnp
from jax import lax
from jax.experimental import pallas as pl
from jax.experimental.pallas import tpu as pltpu
from jax.sharding import PartitionSpec as P

MESH = pl.DeviceIdType.MESH
F32 = jnp.float32
BF16 = jnp.bfloat16

SX, SY, SZ = 4, 4, 8
COLS, ROWS = 2 * SX, SY * SZ
S, NX, NY, NZ = 32, 4, 32, 256
R, B, C = 16, 128, 128
RL = R // COLS
BL = B // COLS
SCALE = 1.0 / (R * B * C)
FAR_FIRST = (4, 5, 3, 2, 6, 7, 1)
XY_ORDER = (10, 6, 9, 11, 14, 2, 5, 7, 8, 13, 15, 1, 3, 4, 12)
ZK_ORDER = (9, 8, 7, 11, 6, 10, 5, 13, 4, 12, 3, 15, 2, 14, 1)
VMEM_BYTES = 40 * 1024 * 1024


def split(a):
    hi = a.astype(BF16)
    lo = (a - hi.astype(F32)).astype(BF16)
    return hi, lo


def dot(a, b):
    return jnp.dot(a, b, preferred_element_type=F32)


def dot_t(a, b):
    return lax.dot_general(a, b, (((1,), (1,)), ((), ())), preferred_element_type=F32)


def add_mod(a, d, n):
    return lax.rem(a + d, n)


def kernel(
    tensor, fy_hbm, fz_hbm, fs_hbm, core_out, gram_out,
    fy, fz, fs, tbuf, send_r, recv_r, core, rows, part, buf_a, buf_b, total, fz_w, fy_w, fs_w,
    mate_in, f_sem, t_sem, s1, r1, s2, r2, so, ro, own_sem, s3, r3, s4, r4, s5, r5,
):
    i = lax.axis_index("row")
    j = lax.axis_index("col")
    y, z = i // SZ, lax.rem(i, SZ)
    x, k = j // 2, lax.rem(j, 2)

    def col_partner(d):
        return add_mod(j, d, COLS)

    def row_partner(d):
        return add_mod(i, d, ROWS)

    loads = [
        pltpu.make_async_copy(tensor.at[:, n], tbuf.at[n], t_sem.at[n]) for n in range(NX)
    ]
    factors = [
        pltpu.make_async_copy(a, b, f_sem.at[n])
        for n, (a, b) in enumerate(((fz_hbm, fz), (fs_hbm, fs), (fy_hbm, fy)))
    ]
    for c in factors[:2] + loads[:1] + factors[2:] + loads[1:]:
        c.start()

    barrier = pltpu.get_barrier_semaphore()

    def greet_col(d, _):
        pl.semaphore_signal(
            barrier, inc=1, device_id=(i, 2 * add_mod(x, d, SX)), device_id_type=MESH
        )
        return 0

    def greet_row(d, _):
        pl.semaphore_signal(
            barrier, inc=1, device_id=(row_partner(d), 2 * x + 1), device_id_type=MESH
        )
        return 0

    for d in range(SX):

        @pl.when(k + d > 0)
        def _():
            greet_col(d, 0)

    lax.fori_loop(1, ROWS, greet_row, 0)

    for c in factors:
        c.wait()
    zh, zl = split(fz[...])
    fz_w[:, :C] = zh
    fz_w[:, C:] = zl
    yh, yl = split(fy[...].T)
    fy_w[:B] = yh
    fy_w[B:] = yl
    sh, sl = split(fs[...])
    pick_r = (
        lax.broadcasted_iota(jnp.int32, (R * 8, R), 0) // 8
        == lax.broadcasted_iota(jnp.int32, (R * 8, R), 1)
    ).astype(F32).astype(BF16)
    pick_s = (
        lax.broadcasted_iota(jnp.int32, (S, S * 8), 1) // 8
        == lax.broadcasted_iota(jnp.int32, (S, S * 8), 0)
    ).astype(F32).astype(BF16)
    same = (
        lax.broadcasted_iota(jnp.int32, (R * 8, S * 8), 0) % 8
        == lax.broadcasted_iota(jnp.int32, (R * 8, S * 8), 1) % 8
    )
    for part_s, at in ((sh, 0), (sl, R * 8)):
        wide = dot(dot(pick_r, part_s).astype(BF16), pick_s)
        fs_w[at : at + R * 8] = jnp.where(same, wide, 0.0).astype(BF16)

    mine_y = pl.ds(pl.multiple_of(j * NY, NY), NY)
    for n in range(NX):
        loads[n].wait()
        for h in range(2):
            t = tbuf[n, :, 16 * h : 16 * h + 16, :].reshape(S * 16, NZ)
            th, tl = split(t)
            u = dot(th, fz_w[...])
            u = u[:, :C] + (u[:, C:] + dot(tl, fz_w[:, :C]))
            u = u.reshape(S, 2, 8, C)
            w = jnp.concatenate([u[:, 0].reshape(S * 8, C), u[:, 1].reshape(S * 8, C)], axis=1)
            wh, wl = split(w)
            v = dot(fs_w[...], wh)
            v = v[: R * 8] + (v[R * 8 :] + dot(fs_w[: R * 8], wl))
            for g in range(2):
                send_r[n, :, 16 * h + 8 * g : 16 * h + 8 * g + 8, :] = v[
                    :, g * C : (g + 1) * C
                ].reshape(R, 8, C)
        if n == 0:

            @pl.when(k == 0)
            def _():
                pl.semaphore_wait(barrier, COLS - 1)
                pl.semaphore_signal(mate_in, inc=1, device_id=(i, j + 1), device_id_type=MESH)

            @pl.when(k == 1)
            def _():
                pl.semaphore_wait(mate_in, 1)

        for rank in range(RL):
            for d in FAR_FIRST:
                q = col_partner(d)
                pltpu.make_async_remote_copy(
                    src_ref=send_r.at[n, q * RL + rank],
                    dst_ref=recv_r.at[n, rank, mine_y, :],
                    send_sem=s1,
                    recv_sem=r1.at[n, rank],
                    device_id=(i, q),
                    device_id_type=MESH,
                ).start()

    @pl.when(k == 1)
    def _():
        pl.semaphore_wait(barrier, 2 * (ROWS - 1))
        pl.semaphore_signal(mate_in, inc=1, device_id=(i, j - 1), device_id_type=MESH)

    for n in range(NX):
        recv_r[n, :, mine_y, :] = send_r[n, pl.ds(j * RL, RL)]

    def block(p):
        return pl.ds(pl.multiple_of(p // RL * 8, 8), 8)

    def at_row(n):
        return pl.ds(pl.multiple_of((i * NX + n) * 8, 8), 8)

    for n in range(NX):
        for rank in range(RL):
            got = recv_r.at[n, rank, pl.ds(0, NY * (COLS - 1)), :]
            pltpu.make_async_copy(got, got, r1.at[n, rank]).wait()
            mh, ml = split(recv_r[n, rank])
            v = dot(fy_w[...], mh)
            core[rank, n] = v[:B] + (v[B:] + dot(fy_w[:B], ml))
            if n == 0 and rank == 0:

                @pl.when(k == 0)
                def _():
                    pl.semaphore_wait(mate_in, 1)

            def send_rows(d, _, n=n, rank=rank):
                p = lax.rem(i // RL + d, ROWS // RL) * RL + rank

                @pl.when(p != i)
                def _():
                    pltpu.make_async_remote_copy(
                        src_ref=core.at[rank, n, block(p), :],
                        dst_ref=rows.at[at_row(n), :],
                        send_sem=s2,
                        recv_sem=r2,
                        device_id=(p, j),
                        device_id_type=MESH,
                    ).start()

                return 0

            lax.fori_loop(0, ROWS // RL, send_rows, 0)
        rows[at_row(n), :] = core[lax.rem(i, RL), n, block(i), :]

    for d in range(1, COLS):
        q = col_partner(d)
        pltpu.make_async_remote_copy(
            src_ref=core.at[:, :, pl.ds(pl.multiple_of(q * BL, BL), BL), :],
            dst_ref=core_out.at[pl.ds(j * RL, RL)],
            send_sem=so,
            recv_sem=ro,
            device_id=(i, q),
            device_id_type=MESH,
        ).start()
    own = pltpu.make_async_copy(
        core.at[:, :, pl.ds(pl.multiple_of(j * BL, BL), BL), :],
        core_out.at[pl.ds(j * RL, RL)],
        own_sem.at[0],
    )
    own.start()

    got = rows.at[pl.ds(0, (ROWS - 1) * NX * 8)]
    pltpu.make_async_copy(got, got, r2).wait()
    gh, gl = [], []
    for e in range(8):
        h, l = split(rows[pl.ds(e, ROWS * NX, stride=8), :])
        gh.append(h)
        gl.append(l)
    gh = jnp.concatenate(gh, axis=1)
    gl = jnp.concatenate(gl, axis=1)
    g = dot_t(jnp.concatenate([gh, gl], axis=0), gh)
    cross = g[128:]
    part[...] = (g[:128] + (cross + cross.T)).reshape(16, 8, 128)

    at_xy, at_zk = x * SY + y, z * 2 + k

    def over_xy(d):
        xx, yy = add_mod(x, d // SY, SX), add_mod(y, d % SY, SY)
        return xx * SY + yy, (yy * SZ + z, xx * 2 + k)

    def over_zk(d):
        zz, kk = add_mod(z, d // 2, SZ), add_mod(k, d % 2, 2)
        return (y * SZ + zz, x * 2 + kk)

    for d in XY_ORDER:
        slot, device = over_xy(d)
        pltpu.make_async_remote_copy(
            src_ref=part.at[slot],
            dst_ref=buf_a.at[at_xy],
            send_sem=s3,
            recv_sem=r3,
            device_id=device,
            device_id_type=MESH,
        ).start()
    buf_a[at_xy] = part[at_xy]
    pltpu.make_async_copy(buf_a.at[pl.ds(0, 15)], buf_a.at[pl.ds(0, 15)], r3).wait()

    buf_b[at_zk] = jnp.sum(buf_a[...], axis=0)
    for d in ZK_ORDER:
        pltpu.make_async_remote_copy(
            src_ref=buf_b.at[at_zk],
            dst_ref=buf_b.at[at_zk],
            send_sem=s4,
            recv_sem=r4,
            device_id=over_zk(d),
            device_id_type=MESH,
        ).start()
    pltpu.make_async_copy(buf_b.at[pl.ds(0, 15)], buf_b.at[pl.ds(0, 15)], r4).wait()
    total[...] = jnp.sum(buf_b[...], axis=0) * SCALE

    for d in XY_ORDER:
        pltpu.make_async_remote_copy(
            src_ref=total,
            dst_ref=gram_out.at[at_xy],
            send_sem=s5,
            recv_sem=r5,
            device_id=over_xy(d)[1],
            device_id_type=MESH,
        ).start()
    own_gram = pltpu.make_async_copy(total, gram_out.at[at_xy], own_sem.at[1])
    own_gram.start()

    sent = send_r.at[:, pl.ds(0, R - RL)]
    pltpu.make_async_copy(sent, sent, s1).wait()
    sent = rows.at[pl.ds(0, (ROWS - 1) * NX * 8)]
    pltpu.make_async_copy(sent, sent, s2).wait()
    sent = core.at[:, :, pl.ds(0, B - BL), :]
    pltpu.make_async_copy(sent, sent, so).wait()
    own.wait()
    own_gram.wait()
    for sem in (s3, s4, s5):
        pltpu.make_async_copy(buf_a.at[pl.ds(0, 15)], buf_a.at[pl.ds(0, 15)], sem).wait()
    got = core_out.at[pl.ds(0, R - RL)]
    pltpu.make_async_copy(got, got, ro).wait()
    pltpu.make_async_copy(gram_out.at[pl.ds(0, 15)], gram_out.at[pl.ds(0, 15)], r5).wait()


def in_hbm(a):
    return pltpu.with_memory_space_constraint(a, pltpu.HBM)


def body(tensor, factor_y, factor_z, factor_s):
    dma = pltpu.SemaphoreType.DMA
    core, gram = pl.pallas_call(
        kernel,
        out_shape=(
            jax.ShapeDtypeStruct((R, NX, BL, C), F32),
            jax.ShapeDtypeStruct((16, 8, 128), F32),
        ),
        in_specs=[pl.BlockSpec(memory_space=pltpu.HBM)] * 4,
        out_specs=(pl.BlockSpec(memory_space=pl.ANY), pl.BlockSpec(memory_space=pl.ANY)),
        scratch_shapes=[
            pltpu.VMEM((NY * COLS, B), F32),
            pltpu.VMEM((NZ, C), F32),
            pltpu.VMEM((R, S), F32),
            pltpu.VMEM((NX, S, NY, NZ), F32),
            pltpu.VMEM((NX, R, NY, C), F32),
            pltpu.VMEM((NX, RL, NY * COLS, C), F32),
            pltpu.VMEM((RL, NX, B, C), F32),
            pltpu.VMEM((ROWS * NX * 8, C), F32),
            pltpu.VMEM((16, 8, 128), F32),
            pltpu.VMEM((16, 8, 128), F32),
            pltpu.VMEM((16, 8, 128), F32),
            pltpu.VMEM((8, 128), F32),
            pltpu.VMEM((NZ, 2 * C), BF16),
            pltpu.VMEM((2 * B, NY * COLS), BF16),
            pltpu.VMEM((2 * R * 8, S * 8), BF16),
            pltpu.SemaphoreType.REGULAR,
            dma((3,)),
            dma((NX,)),
            dma, dma((NX, RL)),
            dma, dma,
            dma, dma, dma((2,)),
            dma, dma,
            dma, dma,
            dma, dma,
        ],
        compiler_params=pltpu.CompilerParams(
            collective_id=0, has_side_effects=True, vmem_limit_bytes=VMEM_BYTES
        ),
    )(*(in_hbm(a) for a in (tensor, factor_y, factor_z, factor_s.T)))
    return core, gram.reshape(128, 128)


def solution(mesh):
    in_specs = (P(None, "row", "col", None), P(), P(), P())
    out_specs = (P(None, "row", "col", None), P())
    return jax.shard_map(body, mesh=mesh, in_specs=in_specs, out_specs=out_specs, check_vma=False)
```

```python
import functools

import jax
import jax.numpy as jnp
from jax import lax
from jax.experimental import pallas as pl
from jax.experimental.pallas import tpu as pltpu
from jax.sharding import PartitionSpec as P

MESH = pl.DeviceIdType.MESH
F32 = jnp.float32
BF16 = jnp.bfloat16

SX, SY, SZ = 4, 4, 8
COLS, ROWS = 2 * SX, SY * SZ
S, NX, NY, NZ = 32, 4, 32, 256
R, B, C = 16, 128, 128
RL = R // COLS
BL = B // COLS
SCALE = 1.0 / (R * B * C)
FAR_FIRST = (4, 5, 3, 2, 6, 7, 1)
XY_ORDER = (10, 6, 9, 11, 14, 2, 5, 7, 8, 13, 15, 1, 3, 4, 12)
ZK_ORDER = (9, 8, 7, 11, 6, 10, 5, 13, 4, 12, 3, 15, 2, 14, 1)
VMEM_BYTES = 40 * 1024 * 1024


def split(a):
    hi = a.astype(BF16)
    lo = (a - hi.astype(F32)).astype(BF16)
    return hi, lo


def dot(a, b):
    return jnp.dot(a, b, preferred_element_type=F32)


def dot_t(a, b):
    return lax.dot_general(a, b, (((1,), (1,)), ((), ())), preferred_element_type=F32)


def add_mod(a, d, n):
    return lax.rem(a + d, n)


def kernel(
    tensor, fy_hbm, fz_hbm, fs_hbm, core_out, gram_out,
    fy, fz, fs, tbuf, send_r, recv_r, core, rows, part, buf_a, buf_b, total, fz_w, fy_w, fs_w,
    mate_in, f_sem, t_sem, s1, r1, s2, r2, so, ro, own_sem, s3, r3, s4, r4, s5, r5,
):
    i = lax.axis_index("row")
    j = lax.axis_index("col")
    y, z = i // SZ, lax.rem(i, SZ)
    x, k = j // 2, lax.rem(j, 2)

    def col_partner(d):
        return add_mod(j, d, COLS)

    def row_partner(d):
        return add_mod(i, d, ROWS)

    loads = [
        pltpu.make_async_copy(tensor.at[:, n], tbuf.at[n], t_sem.at[n]) for n in range(NX)
    ]
    factors = [
        pltpu.make_async_copy(a, b, f_sem.at[n])
        for n, (a, b) in enumerate(((fz_hbm, fz), (fs_hbm, fs), (fy_hbm, fy)))
    ]
    for c in factors[:2] + loads + factors[2:]:
        c.start()

    barrier = pltpu.get_barrier_semaphore()

    def greet_col(d, _):
        pl.semaphore_signal(
            barrier, inc=1, device_id=(i, 2 * add_mod(x, d, SX)), device_id_type=MESH
        )
        return 0

    def greet_row(d, _):
        pl.semaphore_signal(
            barrier, inc=1, device_id=(row_partner(d), 2 * x + 1), device_id_type=MESH
        )
        return 0

    for d in range(SX):

        @pl.when(k + d > 0)
        def _():
            greet_col(d, 0)

    lax.fori_loop(1, ROWS, greet_row, 0)

    for c in factors[:2]:
        c.wait()
    zh, zl = split(fz[...])
    fz_w[:, :C] = zh
    fz_w[:, C:] = zl
    sh, sl = split(fs[...])
    pick_r = (
        lax.broadcasted_iota(jnp.int32, (R * 8, R), 0) // 8
        == lax.broadcasted_iota(jnp.int32, (R * 8, R), 1)
    ).astype(F32).astype(BF16)
    pick_s = (
        lax.broadcasted_iota(jnp.int32, (S, S * 8), 1) // 8
        == lax.broadcasted_iota(jnp.int32, (S, S * 8), 0)
    ).astype(F32).astype(BF16)
    same = (
        lax.broadcasted_iota(jnp.int32, (R * 8, S * 8), 0) % 8
        == lax.broadcasted_iota(jnp.int32, (R * 8, S * 8), 1) % 8
    )
    for part_s, at in ((sh, 0), (sl, R * 8)):
        wide = dot(dot(pick_r, part_s).astype(BF16), pick_s)
        fs_w[at : at + R * 8] = jnp.where(same, wide, 0.0).astype(BF16)

    mine_y = pl.ds(pl.multiple_of(j * NY, NY), NY)
    for n in range(NX):
        loads[n].wait()
        for h in range(2):
            t = tbuf[n, :, 16 * h : 16 * h + 16, :].reshape(S * 16, NZ)
            th, tl = split(t)
            u = dot(th, fz_w[...])
            u = u[:, :C] + (u[:, C:] + dot(tl, fz_w[:, :C]))
            u = u.reshape(S, 2, 8, C)
            w = jnp.concatenate([u[:, 0].reshape(S * 8, C), u[:, 1].reshape(S * 8, C)], axis=1)
            wh, wl = split(w)
            v = dot(fs_w[...], wh)
            v = v[: R * 8] + (v[R * 8 :] + dot(fs_w[: R * 8], wl))
            for g in range(2):
                send_r[n, :, 16 * h + 8 * g : 16 * h + 8 * g + 8, :] = v[
                    :, g * C : (g + 1) * C
                ].reshape(R, 8, C)
        if n == 0:

            @pl.when(k == 0)
            def _():
                pl.semaphore_wait(barrier, COLS - 1)
                pl.semaphore_signal(mate_in, inc=1, device_id=(i, j + 1), device_id_type=MESH)

            @pl.when(k == 1)
            def _():
                pl.semaphore_wait(mate_in, 1)

        for rank in range(RL):
            for d in FAR_FIRST:
                q = col_partner(d)
                pltpu.make_async_remote_copy(
                    src_ref=send_r.at[n, q * RL + rank],
                    dst_ref=recv_r.at[n, rank, mine_y, :],
                    send_sem=s1,
                    recv_sem=r1.at[n, rank],
                    device_id=(i, q),
                    device_id_type=MESH,
                ).start()

    factors[2].wait()
    yh, yl = split(fy[...].T)
    fy_w[:B] = yh
    fy_w[B:] = yl

    @pl.when(k == 1)
    def _():
        pl.semaphore_wait(barrier, 2 * (ROWS - 1))
        pl.semaphore_signal(mate_in, inc=1, device_id=(i, j - 1), device_id_type=MESH)

    for n in range(NX):
        recv_r[n, :, mine_y, :] = send_r[n, pl.ds(j * RL, RL)]

    def block(p):
        return pl.ds(pl.multiple_of(p // RL * 8, 8), 8)

    def at_row(n):
        return pl.ds(pl.multiple_of((i * NX + n) * 8, 8), 8)

    for n in range(NX):
        for rank in range(RL):
            got = recv_r.at[n, rank, pl.ds(0, NY * (COLS - 1)), :]
            pltpu.make_async_copy(got, got, r1.at[n, rank]).wait()
            mh, ml = split(recv_r[n, rank])
            v = dot(fy_w[...], mh)
            core[rank, n] = v[:B] + (v[B:] + dot(fy_w[:B], ml))
            if n == 0 and rank == 0:

                @pl.when(k == 0)
                def _():
                    pl.semaphore_wait(mate_in, 1)

            def send_rows(d, _, n=n, rank=rank):
                p = lax.rem(i // RL + d, ROWS // RL) * RL + rank

                @pl.when(p != i)
                def _():
                    pltpu.make_async_remote_copy(
                        src_ref=core.at[rank, n, block(p), :],
                        dst_ref=rows.at[at_row(n), :],
                        send_sem=s2,
                        recv_sem=r2,
                        device_id=(p, j),
                        device_id_type=MESH,
                    ).start()

                return 0

            lax.fori_loop(0, ROWS // RL, send_rows, 0)
        rows[at_row(n), :] = core[lax.rem(i, RL), n, block(i), :]

    for d in range(1, COLS):
        q = col_partner(d)
        pltpu.make_async_remote_copy(
            src_ref=core.at[:, :, pl.ds(pl.multiple_of(q * BL, BL), BL), :],
            dst_ref=core_out.at[pl.ds(j * RL, RL)],
            send_sem=so,
            recv_sem=ro,
            device_id=(i, q),
            device_id_type=MESH,
        ).start()
    own = pltpu.make_async_copy(
        core.at[:, :, pl.ds(pl.multiple_of(j * BL, BL), BL), :],
        core_out.at[pl.ds(j * RL, RL)],
        own_sem.at[0],
    )
    own.start()

    got = rows.at[pl.ds(0, (ROWS - 1) * NX * 8)]
    pltpu.make_async_copy(got, got, r2).wait()
    gh, gl = [], []
    for e in range(8):
        h, l = split(rows[pl.ds(e, ROWS * NX, stride=8), :])
        gh.append(h)
        gl.append(l)
    gh = jnp.concatenate(gh, axis=1)
    gl = jnp.concatenate(gl, axis=1)
    g = dot_t(jnp.concatenate([gh, gl], axis=0), gh)
    cross = g[128:]
    part[...] = (g[:128] + (cross + cross.T)).reshape(16, 8, 128)

    at_xy, at_zk = x * SY + y, z * 2 + k

    def over_xy(d):
        xx, yy = add_mod(x, d // SY, SX), add_mod(y, d % SY, SY)
        return xx * SY + yy, (yy * SZ + z, xx * 2 + k)

    def over_zk(d):
        zz, kk = add_mod(z, d // 2, SZ), add_mod(k, d % 2, 2)
        return (y * SZ + zz, x * 2 + kk)

    for d in XY_ORDER:
        slot, device = over_xy(d)
        pltpu.make_async_remote_copy(
            src_ref=part.at[slot],
            dst_ref=buf_a.at[at_xy],
            send_sem=s3,
            recv_sem=r3,
            device_id=device,
            device_id_type=MESH,
        ).start()
    buf_a[at_xy] = part[at_xy]
    pltpu.make_async_copy(buf_a.at[pl.ds(0, 15)], buf_a.at[pl.ds(0, 15)], r3).wait()

    buf_b[at_zk] = jnp.sum(buf_a[...], axis=0)
    for d in ZK_ORDER:
        pltpu.make_async_remote_copy(
            src_ref=buf_b.at[at_zk],
            dst_ref=buf_b.at[at_zk],
            send_sem=s4,
            recv_sem=r4,
            device_id=over_zk(d),
            device_id_type=MESH,
        ).start()
    pltpu.make_async_copy(buf_b.at[pl.ds(0, 15)], buf_b.at[pl.ds(0, 15)], r4).wait()
    total[...] = jnp.sum(buf_b[...], axis=0) * SCALE

    for d in XY_ORDER:
        pltpu.make_async_remote_copy(
            src_ref=total,
            dst_ref=gram_out.at[at_xy],
            send_sem=s5,
            recv_sem=r5,
            device_id=over_xy(d)[1],
            device_id_type=MESH,
        ).start()
    own_gram = pltpu.make_async_copy(total, gram_out.at[at_xy], own_sem.at[1])
    own_gram.start()

    sent = send_r.at[:, pl.ds(0, R - RL)]
    pltpu.make_async_copy(sent, sent, s1).wait()
    sent = rows.at[pl.ds(0, (ROWS - 1) * NX * 8)]
    pltpu.make_async_copy(sent, sent, s2).wait()
    sent = core.at[:, :, pl.ds(0, B - BL), :]
    pltpu.make_async_copy(sent, sent, so).wait()
    own.wait()
    own_gram.wait()
    for sem in (s3, s4, s5):
        pltpu.make_async_copy(buf_a.at[pl.ds(0, 15)], buf_a.at[pl.ds(0, 15)], sem).wait()
    got = core_out.at[pl.ds(0, R - RL)]
    pltpu.make_async_copy(got, got, ro).wait()
    pltpu.make_async_copy(gram_out.at[pl.ds(0, 15)], gram_out.at[pl.ds(0, 15)], r5).wait()


def place(core, gram, core_out, gram_out, sem):
    copies = [
        pltpu.make_async_copy(core, core_out, sem.at[0]),
        pltpu.make_async_copy(gram, gram_out, sem.at[1]),
    ]
    for c in copies:
        c.start()
    for c in copies:
        c.wait()


def in_vmem(a):
    return pltpu.with_memory_space_constraint(a, pltpu.VMEM)


def in_hbm(a):
    return pltpu.with_memory_space_constraint(a, pltpu.HBM)


def body(tensor, factor_y, factor_z, factor_s):
    dma = pltpu.SemaphoreType.DMA
    core, gram = pl.pallas_call(
        kernel,
        out_shape=(
            jax.ShapeDtypeStruct((R, NX, BL, C), F32),
            jax.ShapeDtypeStruct((16, 8, 128), F32),
        ),
        in_specs=[pl.BlockSpec(memory_space=pltpu.HBM)] * 4,
        out_specs=(pl.BlockSpec(memory_space=pl.ANY), pl.BlockSpec(memory_space=pl.ANY)),
        scratch_shapes=[
            pltpu.VMEM((NY * COLS, B), F32),
            pltpu.VMEM((NZ, C), F32),
            pltpu.VMEM((R, S), F32),
            pltpu.VMEM((NX, S, NY, NZ), F32),
            pltpu.VMEM((NX, R, NY, C), F32),
            pltpu.VMEM((NX, RL, NY * COLS, C), F32),
            pltpu.VMEM((RL, NX, B, C), F32),
            pltpu.VMEM((ROWS * NX * 8, C), F32),
            pltpu.VMEM((16, 8, 128), F32),
            pltpu.VMEM((16, 8, 128), F32),
            pltpu.VMEM((16, 8, 128), F32),
            pltpu.VMEM((8, 128), F32),
            pltpu.VMEM((NZ, 2 * C), BF16),
            pltpu.VMEM((2 * B, NY * COLS), BF16),
            pltpu.VMEM((2 * R * 8, S * 8), BF16),
            pltpu.SemaphoreType.REGULAR,
            dma((3,)),
            dma((NX,)),
            dma, dma((NX, RL)),
            dma, dma,
            dma, dma, dma((2,)),
            dma, dma,
            dma, dma,
            dma, dma,
        ],
        compiler_params=pltpu.CompilerParams(
            collective_id=0, has_side_effects=True, vmem_limit_bytes=VMEM_BYTES
        ),
    )(*(in_hbm(a) for a in (tensor, factor_y, factor_z, factor_s.T)))
    return pl.pallas_call(
        place,
        out_shape=(
            jax.ShapeDtypeStruct((R, NX, BL, C), F32),
            jax.ShapeDtypeStruct((128, 128), F32),
        ),
        in_specs=[pl.BlockSpec(memory_space=pltpu.VMEM)] * 2,
        out_specs=(pl.BlockSpec(memory_space=pl.ANY), pl.BlockSpec(memory_space=pl.ANY)),
        scratch_shapes=[dma((2,))],
        compiler_params=pltpu.CompilerParams(vmem_limit_bytes=2 * 1024 * 1024),
    )(core, gram.reshape(128, 128))


def solution(mesh):
    in_specs = (P(None, "row", "col", None), P(), P(), P())
    out_specs = (P(None, "row", "col", None), P())
    return jax.shard_map(body, mesh=mesh, in_specs=in_specs, out_specs=out_specs, check_vma=False)
```

```python
import functools

import jax
import jax.numpy as jnp
from jax import lax
from jax.experimental import pallas as pl
from jax.experimental.pallas import tpu as pltpu
from jax.sharding import PartitionSpec as P

MESH = pl.DeviceIdType.MESH
F32 = jnp.float32
BF16 = jnp.bfloat16

SX, SY, SZ = 4, 4, 8
COLS, ROWS = 2 * SX, SY * SZ
S, NX, NY, NZ = 32, 4, 32, 256
R, B, C = 16, 128, 128
RL = R // COLS
BL = B // COLS
SCALE = 1.0 / (R * B * C)
FAR_FIRST = (4, 5, 3, 2, 6, 7, 1)
XY_ORDER = (10, 6, 9, 11, 14, 2, 5, 7, 8, 13, 15, 1, 3, 4, 12)
ZK_ORDER = (9, 8, 7, 11, 6, 10, 5, 13, 4, 12, 3, 15, 2, 14, 1)
VMEM_BYTES = 40 * 1024 * 1024


def split(a):
    hi = a.astype(BF16)
    lo = (a - hi.astype(F32)).astype(BF16)
    return hi, lo


def dot(a, b):
    return jnp.dot(a, b, preferred_element_type=F32)


def dot_t(a, b):
    return lax.dot_general(a, b, (((1,), (1,)), ((), ())), preferred_element_type=F32)


def add_mod(a, d, n):
    return lax.rem(a + d, n)


def kernel(
    tensor, fy_hbm, fz_hbm, fs_hbm, core_out, gram_out,
    fy, fz, fs, tbuf, send_r, recv_r, core, rows, part, buf_a, buf_b, total, fz_w, fy_w, fs_w,
    mate_in, f_sem, t_sem, s1, r1, s2, r2, so, ro, own_sem, s3, r3, s4, r4, s5, r5,
):
    i = lax.axis_index("row")
    j = lax.axis_index("col")
    y, z = i // SZ, lax.rem(i, SZ)
    x, k = j // 2, lax.rem(j, 2)

    def col_partner(d):
        return add_mod(j, d, COLS)

    def row_partner(d):
        return add_mod(i, d, ROWS)

    loads = [
        pltpu.make_async_copy(tensor.at[:, n], tbuf.at[n], t_sem.at[n]) for n in range(NX)
    ]
    factors = [
        pltpu.make_async_copy(a, b, f_sem.at[n])
        for n, (a, b) in enumerate(((fz_hbm, fz), (fs_hbm, fs), (fy_hbm, fy)))
    ]
    for c in factors[:2] + loads + factors[2:]:
        c.start()

    barrier = pltpu.get_barrier_semaphore()

    def greet_col(d, _):
        pl.semaphore_signal(
            barrier, inc=1, device_id=(i, 2 * add_mod(x, d, SX)), device_id_type=MESH
        )
        return 0

    def greet_row(d, _):
        pl.semaphore_signal(
            barrier, inc=1, device_id=(row_partner(d), 2 * x + 1), device_id_type=MESH
        )
        return 0

    for d in range(SX):

        @pl.when(k + d > 0)
        def _():
            greet_col(d, 0)

    lax.fori_loop(1, ROWS, greet_row, 0)

    for c in factors[:2]:
        c.wait()
    zh, zl = split(fz[...])
    fz_w[:, :C] = zh
    fz_w[:, C:] = zl
    sh, sl = split(fs[...])
    pick_r = (
        lax.broadcasted_iota(jnp.int32, (R * 8, R), 0) // 8
        == lax.broadcasted_iota(jnp.int32, (R * 8, R), 1)
    ).astype(F32).astype(BF16)
    pick_s = (
        lax.broadcasted_iota(jnp.int32, (S, S * 8), 1) // 8
        == lax.broadcasted_iota(jnp.int32, (S, S * 8), 0)
    ).astype(F32).astype(BF16)
    same = (
        lax.broadcasted_iota(jnp.int32, (R * 8, S * 8), 0) % 8
        == lax.broadcasted_iota(jnp.int32, (R * 8, S * 8), 1) % 8
    )
    for part_s, at in ((sh, 0), (sl, R * 8)):
        wide = dot(dot(pick_r, part_s).astype(BF16), pick_s)
        fs_w[at : at + R * 8] = jnp.where(same, wide, 0.0).astype(BF16)

    mine_y = pl.ds(pl.multiple_of(j * NY, NY), NY)
    for n in range(NX):
        loads[n].wait()
        for h in range(2):
            t = tbuf[n, :, 16 * h : 16 * h + 16, :].reshape(S * 16, NZ)
            th, tl = split(t)
            u = dot(th, fz_w[...])
            u = u[:, :C] + (u[:, C:] + dot(tl, fz_w[:, :C]))
            u = u.reshape(S, 2, 8, C)
            w = jnp.concatenate([u[:, 0].reshape(S * 8, C), u[:, 1].reshape(S * 8, C)], axis=1)
            wh, wl = split(w)
            v = dot(fs_w[...], wh)
            v = v[: R * 8] + (v[R * 8 :] + dot(fs_w[: R * 8], wl))
            for g in range(2):
                send_r[n, :, 16 * h + 8 * g : 16 * h + 8 * g + 8, :] = v[
                    :, g * C : (g + 1) * C
                ].reshape(R, 8, C)
        if n == 0:

            @pl.when(k == 0)
            def _():
                pl.semaphore_wait(barrier, COLS - 1)
                pl.semaphore_signal(mate_in, inc=1, device_id=(i, j + 1), device_id_type=MESH)

            @pl.when(k == 1)
            def _():
                pl.semaphore_wait(mate_in, 1)

        for rank in range(RL):
            for d in FAR_FIRST:
                q = col_partner(d)
                pltpu.make_async_remote_copy(
                    src_ref=send_r.at[n, q * RL + rank],
                    dst_ref=recv_r.at[n, rank, mine_y, :],
                    send_sem=s1,
                    recv_sem=r1.at[n, rank],
                    device_id=(i, q),
                    device_id_type=MESH,
                ).start()

    factors[2].wait()
    yh, yl = split(fy[...].T)
    fy_w[:B] = yh
    fy_w[B:] = yl

    @pl.when(k == 1)
    def _():
        pl.semaphore_wait(barrier, 2 * (ROWS - 1))
        pl.semaphore_signal(mate_in, inc=1, device_id=(i, j - 1), device_id_type=MESH)

    for n in range(NX):
        recv_r[n, :, mine_y, :] = send_r[n, pl.ds(j * RL, RL)]

    def block(p):
        return pl.ds(pl.multiple_of(p // RL * 8, 8), 8)

    def at_row(n):
        return pl.ds(pl.multiple_of((i * NX + n) * 8, 8), 8)

    @pl.when(k == 0)
    def _():
        pl.semaphore_wait(mate_in, 1)

    def finish(c, _):
        n, rank = c // RL, lax.rem(c, RL)
        got = recv_r.at[n, rank, pl.ds(0, NY * (COLS - 1)), :]
        pltpu.make_async_copy(got, got, r1.at[n, rank]).wait()
        mh, ml = split(recv_r[n, rank])
        v = dot(fy_w[...], mh)
        core[rank, n] = v[:B] + (v[B:] + dot(fy_w[:B], ml))

        def send_rows(d, _):
            p = lax.rem(i // RL + d, ROWS // RL) * RL + rank

            @pl.when(p != i)
            def _():
                pltpu.make_async_remote_copy(
                    src_ref=core.at[rank, n, block(p), :],
                    dst_ref=rows.at[at_row(n), :],
                    send_sem=s2,
                    recv_sem=r2,
                    device_id=(p, j),
                    device_id_type=MESH,
                ).start()

            return 0

        lax.fori_loop(0, ROWS // RL, send_rows, 0)
        return 0

    lax.fori_loop(0, NX * RL, finish, 0)
    for n in range(NX):
        rows[at_row(n), :] = core[lax.rem(i, RL), n, block(i), :]

    for d in range(1, COLS):
        q = col_partner(d)
        pltpu.make_async_remote_copy(
            src_ref=core.at[:, :, pl.ds(pl.multiple_of(q * BL, BL), BL), :],
            dst_ref=core_out.at[pl.ds(j * RL, RL)],
            send_sem=so,
            recv_sem=ro,
            device_id=(i, q),
            device_id_type=MESH,
        ).start()
    own = pltpu.make_async_copy(
        core.at[:, :, pl.ds(pl.multiple_of(j * BL, BL), BL), :],
        core_out.at[pl.ds(j * RL, RL)],
        own_sem.at[0],
    )
    own.start()

    got = rows.at[pl.ds(0, (ROWS - 1) * NX * 8)]
    pltpu.make_async_copy(got, got, r2).wait()
    gh, gl = [], []
    for e in range(8):
        h, l = split(rows[pl.ds(e, ROWS * NX, stride=8), :])
        gh.append(h)
        gl.append(l)
    gh = jnp.concatenate(gh, axis=1)
    gl = jnp.concatenate(gl, axis=1)
    g = dot_t(jnp.concatenate([gh, gl], axis=0), gh)
    cross = g[128:]
    part[...] = (g[:128] + (cross + cross.T)).reshape(16, 8, 128)

    at_xy, at_zk = x * SY + y, z * 2 + k

    def over_xy(d):
        xx, yy = add_mod(x, d // SY, SX), add_mod(y, d % SY, SY)
        return xx * SY + yy, (yy * SZ + z, xx * 2 + k)

    def over_zk(d):
        zz, kk = add_mod(z, d // 2, SZ), add_mod(k, d % 2, 2)
        return (y * SZ + zz, x * 2 + kk)

    for d in XY_ORDER:
        slot, device = over_xy(d)
        pltpu.make_async_remote_copy(
            src_ref=part.at[slot],
            dst_ref=buf_a.at[at_xy],
            send_sem=s3,
            recv_sem=r3,
            device_id=device,
            device_id_type=MESH,
        ).start()
    buf_a[at_xy] = part[at_xy]
    pltpu.make_async_copy(buf_a.at[pl.ds(0, 15)], buf_a.at[pl.ds(0, 15)], r3).wait()

    buf_b[at_zk] = jnp.sum(buf_a[...], axis=0)
    for d in ZK_ORDER:
        pltpu.make_async_remote_copy(
            src_ref=buf_b.at[at_zk],
            dst_ref=buf_b.at[at_zk],
            send_sem=s4,
            recv_sem=r4,
            device_id=over_zk(d),
            device_id_type=MESH,
        ).start()
    pltpu.make_async_copy(buf_b.at[pl.ds(0, 15)], buf_b.at[pl.ds(0, 15)], r4).wait()
    total[...] = jnp.sum(buf_b[...], axis=0) * SCALE

    for d in XY_ORDER:
        pltpu.make_async_remote_copy(
            src_ref=total,
            dst_ref=gram_out.at[at_xy],
            send_sem=s5,
            recv_sem=r5,
            device_id=over_xy(d)[1],
            device_id_type=MESH,
        ).start()
    own_gram = pltpu.make_async_copy(total, gram_out.at[at_xy], own_sem.at[1])
    own_gram.start()

    sent = send_r.at[:, pl.ds(0, R - RL)]
    pltpu.make_async_copy(sent, sent, s1).wait()
    sent = rows.at[pl.ds(0, (ROWS - 1) * NX * 8)]
    pltpu.make_async_copy(sent, sent, s2).wait()
    sent = core.at[:, :, pl.ds(0, B - BL), :]
    pltpu.make_async_copy(sent, sent, so).wait()
    own.wait()
    own_gram.wait()
    for sem in (s3, s4, s5):
        pltpu.make_async_copy(buf_a.at[pl.ds(0, 15)], buf_a.at[pl.ds(0, 15)], sem).wait()
    got = core_out.at[pl.ds(0, R - RL)]
    pltpu.make_async_copy(got, got, ro).wait()
    pltpu.make_async_copy(gram_out.at[pl.ds(0, 15)], gram_out.at[pl.ds(0, 15)], r5).wait()


def place(core, gram, core_out, gram_out, sem):
    copies = [
        pltpu.make_async_copy(core, core_out, sem.at[0]),
        pltpu.make_async_copy(gram, gram_out, sem.at[1]),
    ]
    for c in copies:
        c.start()
    for c in copies:
        c.wait()


def in_vmem(a):
    return pltpu.with_memory_space_constraint(a, pltpu.VMEM)


def in_hbm(a):
    return pltpu.with_memory_space_constraint(a, pltpu.HBM)


def body(tensor, factor_y, factor_z, factor_s):
    dma = pltpu.SemaphoreType.DMA
    core, gram = pl.pallas_call(
        kernel,
        out_shape=(
            jax.ShapeDtypeStruct((R, NX, BL, C), F32),
            jax.ShapeDtypeStruct((16, 8, 128), F32),
        ),
        in_specs=[pl.BlockSpec(memory_space=pltpu.HBM)] * 4,
        out_specs=(pl.BlockSpec(memory_space=pl.ANY), pl.BlockSpec(memory_space=pl.ANY)),
        scratch_shapes=[
            pltpu.VMEM((NY * COLS, B), F32),
            pltpu.VMEM((NZ, C), F32),
            pltpu.VMEM((R, S), F32),
            pltpu.VMEM((NX, S, NY, NZ), F32),
            pltpu.VMEM((NX, R, NY, C), F32),
            pltpu.VMEM((NX, RL, NY * COLS, C), F32),
            pltpu.VMEM((RL, NX, B, C), F32),
            pltpu.VMEM((ROWS * NX * 8, C), F32),
            pltpu.VMEM((16, 8, 128), F32),
            pltpu.VMEM((16, 8, 128), F32),
            pltpu.VMEM((16, 8, 128), F32),
            pltpu.VMEM((8, 128), F32),
            pltpu.VMEM((NZ, 2 * C), BF16),
            pltpu.VMEM((2 * B, NY * COLS), BF16),
            pltpu.VMEM((2 * R * 8, S * 8), BF16),
            pltpu.SemaphoreType.REGULAR,
            dma((3,)),
            dma((NX,)),
            dma, dma((NX, RL)),
            dma, dma,
            dma, dma, dma((2,)),
            dma, dma,
            dma, dma,
            dma, dma,
        ],
        compiler_params=pltpu.CompilerParams(
            collective_id=0, has_side_effects=True, vmem_limit_bytes=VMEM_BYTES
        ),
    )(*(in_hbm(a) for a in (tensor, factor_y, factor_z, factor_s.T)))
    return pl.pallas_call(
        place,
        out_shape=(
            jax.ShapeDtypeStruct((R, NX, BL, C), F32),
            jax.ShapeDtypeStruct((128, 128), F32),
        ),
        in_specs=[pl.BlockSpec(memory_space=pltpu.VMEM)] * 2,
        out_specs=(pl.BlockSpec(memory_space=pl.ANY), pl.BlockSpec(memory_space=pl.ANY)),
        scratch_shapes=[dma((2,))],
        compiler_params=pltpu.CompilerParams(vmem_limit_bytes=2 * 1024 * 1024),
    )(core, gram.reshape(128, 128))


def solution(mesh):
    in_specs = (P(None, "row", "col", None), P(), P(), P())
    out_specs = (P(None, "row", "col", None), P())
    return jax.shard_map(body, mesh=mesh, in_specs=in_specs, out_specs=out_specs, check_vma=False)
```

```python
import functools

import jax
import jax.numpy as jnp
from jax import lax
from jax.experimental import pallas as pl
from jax.experimental.pallas import tpu as pltpu
from jax.sharding import PartitionSpec as P

MESH = pl.DeviceIdType.MESH
F32 = jnp.float32
BF16 = jnp.bfloat16

SX, SY, SZ = 4, 4, 8
COLS, ROWS = 2 * SX, SY * SZ
S, NX, NY, NZ = 32, 4, 32, 256
R, B, C = 16, 128, 128
RL = R // COLS
BL = B // COLS
SCALE = 1.0 / (R * B * C)
FAR_FIRST = (4, 5, 3, 2, 6, 7, 1)
XY_ORDER = (10, 6, 9, 11, 14, 2, 5, 7, 8, 13, 15, 1, 3, 4, 12)
ZK_ORDER = (9, 8, 7, 11, 6, 10, 5, 13, 4, 12, 3, 15, 2, 14, 1)
VMEM_BYTES = 40 * 1024 * 1024


def split(a):
    hi = a.astype(BF16)
    lo = (a - hi.astype(F32)).astype(BF16)
    return hi, lo


def dot(a, b):
    return jnp.dot(a, b, preferred_element_type=F32)


def dot_t(a, b):
    return lax.dot_general(a, b, (((1,), (1,)), ((), ())), preferred_element_type=F32)


def add_mod(a, d, n):
    return jnp.where(a + d < n, a + d, a + d - n)


def kernel(
    tensor, fy_hbm, fz_hbm, fs_hbm, core_out, gram_out,
    fy, fz, fs, tbuf, send_r, recv_r, core, rows, part, buf_a, buf_b, total, fz_w, fy_w, fs_w,
    mate_in, f_sem, t_sem, s1, r1, s2, r2, so, ro, own_sem, s3, r3, s4, r4, s5, r5,
):
    i = lax.axis_index("row")
    j = lax.axis_index("col")
    y, z = i // SZ, lax.rem(i, SZ)
    x, k = j // 2, lax.rem(j, 2)

    def col_partner(d):
        return add_mod(j, d, COLS)

    def row_partner(d):
        return add_mod(i, d, ROWS)

    loads = [
        pltpu.make_async_copy(tensor.at[:, n], tbuf.at[n], t_sem.at[n]) for n in range(NX)
    ]
    factors = [
        pltpu.make_async_copy(a, b, f_sem.at[n])
        for n, (a, b) in enumerate(((fz_hbm, fz), (fs_hbm, fs), (fy_hbm, fy)))
    ]
    for c in factors[:2] + loads + factors[2:]:
        c.start()

    barrier = pltpu.get_barrier_semaphore()

    def greet_col(d, _):
        pl.semaphore_signal(
            barrier, inc=1, device_id=(i, 2 * add_mod(x, d, SX)), device_id_type=MESH
        )
        return 0

    def greet_row(d, _):
        pl.semaphore_signal(
            barrier, inc=1, device_id=(row_partner(d), 2 * x + 1), device_id_type=MESH
        )
        return 0

    for d in range(SX):

        @pl.when(k + d > 0)
        def _():
            greet_col(d, 0)

    lax.fori_loop(1, ROWS, greet_row, 0)

    for c in factors[:2]:
        c.wait()
    zh, zl = split(fz[...])
    fz_w[:, :C] = zh
    fz_w[:, C:] = zl
    sh, sl = split(fs[...])
    pick_r = (
        lax.broadcasted_iota(jnp.int32, (R * 8, R), 0) // 8
        == lax.broadcasted_iota(jnp.int32, (R * 8, R), 1)
    ).astype(F32).astype(BF16)
    pick_s = (
        lax.broadcasted_iota(jnp.int32, (S, S * 8), 1) // 8
        == lax.broadcasted_iota(jnp.int32, (S, S * 8), 0)
    ).astype(F32).astype(BF16)
    same = (
        lax.broadcasted_iota(jnp.int32, (R * 8, S * 8), 0) % 8
        == lax.broadcasted_iota(jnp.int32, (R * 8, S * 8), 1) % 8
    )
    for part_s, at in ((sh, 0), (sl, R * 8)):
        wide = dot(dot(pick_r, part_s).astype(BF16), pick_s)
        fs_w[at : at + R * 8] = jnp.where(same, wide, 0.0).astype(BF16)

    mine_y = pl.ds(pl.multiple_of(j * NY, NY), NY)
    def contract(n):
        pltpu.make_async_copy(tensor.at[:, n], tbuf.at[n], t_sem.at[n]).wait()
        for h in range(2):
            t = tbuf[n, :, 16 * h : 16 * h + 16, :].reshape(S * 16, NZ)
            th, tl = split(t)
            u = dot(th, fz_w[...])
            u = u[:, :C] + (u[:, C:] + dot(tl, fz_w[:, :C]))
            u = u.reshape(S, 2, 8, C)
            w = jnp.concatenate([u[:, 0].reshape(S * 8, C), u[:, 1].reshape(S * 8, C)], axis=1)
            wh, wl = split(w)
            v = dot(fs_w[...], wh)
            v = v[: R * 8] + (v[R * 8 :] + dot(fs_w[: R * 8], wl))
            for g in range(2):
                send_r[n, :, 16 * h + 8 * g : 16 * h + 8 * g + 8, :] = v[
                    :, g * C : (g + 1) * C
                ].reshape(R, 8, C)

    def send_ranks(n):
        for rank in range(RL):
            for d in FAR_FIRST:
                q = col_partner(d)
                pltpu.make_async_remote_copy(
                    src_ref=send_r.at[n, q * RL + rank],
                    dst_ref=recv_r.at[n, rank, mine_y, :],
                    send_sem=s1,
                    recv_sem=r1.at[n, rank],
                    device_id=(i, q),
                    device_id_type=MESH,
                ).start()

    contract(0)

    @pl.when(k == 0)
    def _():
        pl.semaphore_wait(barrier, COLS - 1)
        pl.semaphore_signal(mate_in, inc=1, device_id=(i, j + 1), device_id_type=MESH)

    @pl.when(k == 1)
    def _():
        pl.semaphore_wait(mate_in, 1)

    send_ranks(0)

    def rest(n, _):
        contract(n)
        send_ranks(n)
        return 0

    lax.fori_loop(1, NX, rest, 0)

    factors[2].wait()
    yh, yl = split(fy[...].T)
    fy_w[:B] = yh
    fy_w[B:] = yl

    @pl.when(k == 1)
    def _():
        pl.semaphore_wait(barrier, 2 * (ROWS - 1))
        pl.semaphore_signal(mate_in, inc=1, device_id=(i, j - 1), device_id_type=MESH)

    for n in range(NX):
        recv_r[n, :, mine_y, :] = send_r[n, pl.ds(j * RL, RL)]

    def block(p):
        return pl.ds(pl.multiple_of(p // RL * 8, 8), 8)

    def at_row(n):
        return pl.ds(pl.multiple_of((i * NX + n) * 8, 8), 8)

    @pl.when(k == 0)
    def _():
        pl.semaphore_wait(mate_in, 1)

    def finish(c, _):
        n, rank = c // RL, lax.rem(c, RL)
        got = recv_r.at[n, rank, pl.ds(0, NY * (COLS - 1)), :]
        pltpu.make_async_copy(got, got, r1.at[n, rank]).wait()
        mh, ml = split(recv_r[n, rank])
        v = dot(fy_w[...], mh)
        core[rank, n] = v[:B] + (v[B:] + dot(fy_w[:B], ml))

        def send_rows(d, _):
            slot = add_mod(i // RL, d, ROWS // RL)
            p = slot * RL + rank

            @pl.when(p != i)
            def _():
                pltpu.make_async_remote_copy(
                    src_ref=core.at[rank, n, pl.ds(pl.multiple_of(slot * 8, 8), 8), :],
                    dst_ref=rows.at[at_row(n), :],
                    send_sem=s2,
                    recv_sem=r2,
                    device_id=(p, j),
                    device_id_type=MESH,
                ).start()

            return 0

        lax.fori_loop(0, ROWS // RL, send_rows, 0)
        return 0

    lax.fori_loop(0, NX * RL, finish, 0)
    for n in range(NX):
        rows[at_row(n), :] = core[lax.rem(i, RL), n, block(i), :]

    for d in range(1, COLS):
        q = col_partner(d)
        pltpu.make_async_remote_copy(
            src_ref=core.at[:, :, pl.ds(pl.multiple_of(q * BL, BL), BL), :],
            dst_ref=core_out.at[pl.ds(j * RL, RL)],
            send_sem=so,
            recv_sem=ro,
            device_id=(i, q),
            device_id_type=MESH,
        ).start()
    own = pltpu.make_async_copy(
        core.at[:, :, pl.ds(pl.multiple_of(j * BL, BL), BL), :],
        core_out.at[pl.ds(j * RL, RL)],
        own_sem.at[0],
    )
    own.start()

    got = rows.at[pl.ds(0, (ROWS - 1) * NX * 8)]
    pltpu.make_async_copy(got, got, r2).wait()
    gh, gl = [], []
    for e in range(8):
        h, l = split(rows[pl.ds(e, ROWS * NX, stride=8), :])
        gh.append(h)
        gl.append(l)
    gh = jnp.concatenate(gh, axis=1)
    gl = jnp.concatenate(gl, axis=1)
    g = dot_t(jnp.concatenate([gh, gl], axis=0), gh)
    cross = g[128:]
    part[...] = (g[:128] + (cross + cross.T)).reshape(16, 8, 128)

    at_xy, at_zk = x * SY + y, z * 2 + k

    def over_xy(d):
        xx, yy = add_mod(x, d // SY, SX), add_mod(y, d % SY, SY)
        return xx * SY + yy, (yy * SZ + z, xx * 2 + k)

    def over_zk(d):
        zz, kk = add_mod(z, d // 2, SZ), add_mod(k, d % 2, 2)
        return (y * SZ + zz, x * 2 + kk)

    for d in XY_ORDER:
        slot, device = over_xy(d)
        pltpu.make_async_remote_copy(
            src_ref=part.at[slot],
            dst_ref=buf_a.at[at_xy],
            send_sem=s3,
            recv_sem=r3,
            device_id=device,
            device_id_type=MESH,
        ).start()
    buf_a[at_xy] = part[at_xy]
    pltpu.make_async_copy(buf_a.at[pl.ds(0, 15)], buf_a.at[pl.ds(0, 15)], r3).wait()

    buf_b[at_zk] = jnp.sum(buf_a[...], axis=0)
    for d in ZK_ORDER:
        pltpu.make_async_remote_copy(
            src_ref=buf_b.at[at_zk],
            dst_ref=buf_b.at[at_zk],
            send_sem=s4,
            recv_sem=r4,
            device_id=over_zk(d),
            device_id_type=MESH,
        ).start()
    pltpu.make_async_copy(buf_b.at[pl.ds(0, 15)], buf_b.at[pl.ds(0, 15)], r4).wait()
    total[...] = jnp.sum(buf_b[...], axis=0) * SCALE

    for d in XY_ORDER:
        pltpu.make_async_remote_copy(
            src_ref=total,
            dst_ref=gram_out.at[at_xy],
            send_sem=s5,
            recv_sem=r5,
            device_id=over_xy(d)[1],
            device_id_type=MESH,
        ).start()
    own_gram = pltpu.make_async_copy(total, gram_out.at[at_xy], own_sem.at[1])
    own_gram.start()

    sent = send_r.at[:, pl.ds(0, R - RL)]
    pltpu.make_async_copy(sent, sent, s1).wait()
    sent = rows.at[pl.ds(0, (ROWS - 1) * NX * 8)]
    pltpu.make_async_copy(sent, sent, s2).wait()
    sent = core.at[:, :, pl.ds(0, B - BL), :]
    pltpu.make_async_copy(sent, sent, so).wait()
    own.wait()
    own_gram.wait()
    for sem in (s3, s4, s5):
        pltpu.make_async_copy(buf_a.at[pl.ds(0, 15)], buf_a.at[pl.ds(0, 15)], sem).wait()
    got = core_out.at[pl.ds(0, R - RL)]
    pltpu.make_async_copy(got, got, ro).wait()
    pltpu.make_async_copy(gram_out.at[pl.ds(0, 15)], gram_out.at[pl.ds(0, 15)], r5).wait()


def place(core, gram, core_out, gram_out, sem):
    copies = [
        pltpu.make_async_copy(core, core_out, sem.at[0]),
        pltpu.make_async_copy(gram, gram_out, sem.at[1]),
    ]
    for c in copies:
        c.start()
    for c in copies:
        c.wait()


def in_vmem(a):
    return pltpu.with_memory_space_constraint(a, pltpu.VMEM)


def in_hbm(a):
    return pltpu.with_memory_space_constraint(a, pltpu.HBM)


def body(tensor, factor_y, factor_z, factor_s):
    dma = pltpu.SemaphoreType.DMA
    core, gram = pl.pallas_call(
        kernel,
        out_shape=(
            jax.ShapeDtypeStruct((R, NX, BL, C), F32),
            jax.ShapeDtypeStruct((16, 8, 128), F32),
        ),
        in_specs=[pl.BlockSpec(memory_space=pltpu.HBM)] * 4,
        out_specs=(pl.BlockSpec(memory_space=pl.ANY), pl.BlockSpec(memory_space=pl.ANY)),
        scratch_shapes=[
            pltpu.VMEM((NY * COLS, B), F32),
            pltpu.VMEM((NZ, C), F32),
            pltpu.VMEM((R, S), F32),
            pltpu.VMEM((NX, S, NY, NZ), F32),
            pltpu.VMEM((NX, R, NY, C), F32),
            pltpu.VMEM((NX, RL, NY * COLS, C), F32),
            pltpu.VMEM((RL, NX, B, C), F32),
            pltpu.VMEM((ROWS * NX * 8, C), F32),
            pltpu.VMEM((16, 8, 128), F32),
            pltpu.VMEM((16, 8, 128), F32),
            pltpu.VMEM((16, 8, 128), F32),
            pltpu.VMEM((8, 128), F32),
            pltpu.VMEM((NZ, 2 * C), BF16),
            pltpu.VMEM((2 * B, NY * COLS), BF16),
            pltpu.VMEM((2 * R * 8, S * 8), BF16),
            pltpu.SemaphoreType.REGULAR,
            dma((3,)),
            dma((NX,)),
            dma, dma((NX, RL)),
            dma, dma,
            dma, dma, dma((2,)),
            dma, dma,
            dma, dma,
            dma, dma,
        ],
        compiler_params=pltpu.CompilerParams(
            collective_id=0, has_side_effects=True, vmem_limit_bytes=VMEM_BYTES
        ),
    )(*(in_hbm(a) for a in (tensor, factor_y, factor_z, factor_s.T)))
    return pl.pallas_call(
        place,
        out_shape=(
            jax.ShapeDtypeStruct((R, NX, BL, C), F32),
            jax.ShapeDtypeStruct((128, 128), F32),
        ),
        in_specs=[pl.BlockSpec(memory_space=pltpu.VMEM)] * 2,
        out_specs=(pl.BlockSpec(memory_space=pl.ANY), pl.BlockSpec(memory_space=pl.ANY)),
        scratch_shapes=[dma((2,))],
        compiler_params=pltpu.CompilerParams(vmem_limit_bytes=2 * 1024 * 1024),
    )(core, gram.reshape(128, 128))


def solution(mesh):
    in_specs = (P(None, "row", "col", None), P(), P(), P())
    out_specs = (P(None, "row", "col", None), P())
    return jax.shard_map(body, mesh=mesh, in_specs=in_specs, out_specs=out_specs, check_vma=False)
```

```python
import functools

import jax
import jax.numpy as jnp
from jax import lax
from jax.experimental import pallas as pl
from jax.experimental.pallas import tpu as pltpu
from jax.sharding import PartitionSpec as P

MESH = pl.DeviceIdType.MESH
F32 = jnp.float32
BF16 = jnp.bfloat16

SX, SY, SZ = 4, 4, 8
COLS, ROWS = 2 * SX, SY * SZ
S, NX, NY, NZ = 32, 4, 32, 256
R, B, C = 16, 128, 128
RL = R // COLS
BL = B // COLS
SCALE = 1.0 / (R * B * C)
FAR_FIRST = (4, 5, 3, 2, 6, 7, 1)
XY_ORDER = (10, 6, 9, 11, 14, 2, 5, 7, 8, 13, 15, 1, 3, 4, 12)
ZK_ORDER = (9, 8, 7, 11, 6, 10, 5, 13, 4, 12, 3, 15, 2, 14, 1)
VMEM_BYTES = 40 * 1024 * 1024


def split(a):
    hi = a.astype(BF16)
    lo = (a - hi.astype(F32)).astype(BF16)
    return hi, lo


def dot(a, b):
    return jnp.dot(a, b, preferred_element_type=F32)


def dot_t(a, b):
    return lax.dot_general(a, b, (((1,), (1,)), ((), ())), preferred_element_type=F32)


def add_mod(a, d, n):
    return jnp.where(a + d < n, a + d, a + d - n)


def kernel(
    tensor, fy_hbm, fz_hbm, fs_hbm, core_out, gram_out,
    fy, fz, fs, tbuf, send_r, recv_r, core, rows, part, buf_a, buf_b, total, fz_w, fy_w, fs_w,
    mate_in, f_sem, t_sem, s1, r1, s2, r2, so, ro, own_sem, s3, r3, s4, r4, s5, r5,
):
    i = lax.axis_index("row")
    j = lax.axis_index("col")
    y, z = i // SZ, lax.rem(i, SZ)
    x, k = j // 2, lax.rem(j, 2)

    def col_partner(d):
        return add_mod(j, d, COLS)

    def row_partner(d):
        return add_mod(i, d, ROWS)

    loads = [
        pltpu.make_async_copy(tensor.at[:, n], tbuf.at[n], t_sem.at[n]) for n in range(NX)
    ]
    factors = [
        pltpu.make_async_copy(a, b, f_sem.at[n])
        for n, (a, b) in enumerate(((fz_hbm, fz), (fs_hbm, fs), (fy_hbm, fy)))
    ]
    for c in factors[:2] + loads + factors[2:]:
        c.start()

    barrier = pltpu.get_barrier_semaphore()

    def greet_col(d, _):
        pl.semaphore_signal(
            barrier, inc=1, device_id=(i, 2 * add_mod(x, d, SX)), device_id_type=MESH
        )
        return 0

    def greet_row(d, _):
        pl.semaphore_signal(
            barrier, inc=1, device_id=(row_partner(d), 2 * x + 1), device_id_type=MESH
        )
        return 0

    for d in range(SX):

        @pl.when(k + d > 0)
        def _():
            greet_col(d, 0)

    lax.fori_loop(1, ROWS, greet_row, 0)

    for c in factors[:2]:
        c.wait()
    zh, zl = split(fz[...])
    fz_w[:, :C] = zh
    fz_w[:, C:] = zl
    sh, sl = split(fs[...])
    pick_r = (
        lax.broadcasted_iota(jnp.int32, (R * 8, R), 0) // 8
        == lax.broadcasted_iota(jnp.int32, (R * 8, R), 1)
    ).astype(F32).astype(BF16)
    pick_s = (
        lax.broadcasted_iota(jnp.int32, (S, S * 8), 1) // 8
        == lax.broadcasted_iota(jnp.int32, (S, S * 8), 0)
    ).astype(F32).astype(BF16)
    same = (
        lax.broadcasted_iota(jnp.int32, (R * 8, S * 8), 0) % 8
        == lax.broadcasted_iota(jnp.int32, (R * 8, S * 8), 1) % 8
    )
    for part_s, at in ((sh, 0), (sl, R * 8)):
        wide = dot(dot(pick_r, part_s).astype(BF16), pick_s)
        fs_w[at : at + R * 8] = jnp.where(same, wide, 0.0).astype(BF16)

    mine_y = pl.ds(pl.multiple_of(j * NY, NY), NY)
    def contract(n):
        pltpu.make_async_copy(tensor.at[:, n], tbuf.at[n], t_sem.at[n]).wait()
        for h in range(2):
            t = tbuf[n, :, 16 * h : 16 * h + 16, :].reshape(S * 16, NZ)
            th, tl = split(t)
            u = dot(th, fz_w[...])
            u = u[:, :C] + (u[:, C:] + dot(tl, fz_w[:, :C]))
            u = u.reshape(S, 2, 8, C)
            w = jnp.concatenate([u[:, 0].reshape(S * 8, C), u[:, 1].reshape(S * 8, C)], axis=1)
            wh, wl = split(w)
            v = dot(fs_w[...], wh)
            v = v[: R * 8] + (v[R * 8 :] + dot(fs_w[: R * 8], wl))
            for g in range(2):
                send_r[n, :, 16 * h + 8 * g : 16 * h + 8 * g + 8, :] = v[
                    :, g * C : (g + 1) * C
                ].reshape(R, 8, C)

    def send_ranks(n):
        for rank in range(RL):
            for d in FAR_FIRST:
                q = col_partner(d)
                pltpu.make_async_remote_copy(
                    src_ref=send_r.at[n, q * RL + rank],
                    dst_ref=recv_r.at[n, rank, mine_y, :],
                    send_sem=s1,
                    recv_sem=r1.at[n, rank],
                    device_id=(i, q),
                    device_id_type=MESH,
                ).start()

    contract(0)

    @pl.when(k == 0)
    def _():
        pl.semaphore_wait(barrier, COLS - 1)
        pl.semaphore_signal(mate_in, inc=1, device_id=(i, j + 1), device_id_type=MESH)

    @pl.when(k == 1)
    def _():
        pl.semaphore_wait(mate_in, 1)

    send_ranks(0)

    def rest(n, _):
        contract(n)
        send_ranks(n)
        return 0

    lax.fori_loop(1, NX, rest, 0)

    factors[2].wait()
    yh, yl = split(fy[...].T)
    fy_w[:B] = yh
    fy_w[B:] = yl

    @pl.when(k == 1)
    def _():
        pl.semaphore_wait(barrier, 2 * (ROWS - 1))
        pl.semaphore_signal(mate_in, inc=1, device_id=(i, j - 1), device_id_type=MESH)

    for n in range(NX):
        recv_r[n, :, mine_y, :] = send_r[n, pl.ds(j * RL, RL)]

    def block(p):
        return pl.ds(pl.multiple_of(p // RL * 8, 8), 8)

    def at_row(n):
        return pl.ds(pl.multiple_of((i * NX + n) * 8, 8), 8)

    def finish(c, _):
        n, rank = c // RL, lax.rem(c, RL)
        got = recv_r.at[n, rank, pl.ds(0, NY * (COLS - 1)), :]
        pltpu.make_async_copy(got, got, r1.at[n, rank]).wait()
        mh, ml = split(recv_r[n, rank])
        v = dot(fy_w[...], mh)
        core[rank, n] = v[:B] + (v[B:] + dot(fy_w[:B], ml))

        @pl.when((k == 0) & (c == 0))
        def _():
            pl.semaphore_wait(mate_in, 1)

        def send_rows(d, _):
            slot = add_mod(i // RL, d, ROWS // RL)
            p = slot * RL + rank

            @pl.when(p != i)
            def _():
                pltpu.make_async_remote_copy(
                    src_ref=core.at[rank, n, pl.ds(pl.multiple_of(slot * 8, 8), 8), :],
                    dst_ref=rows.at[at_row(n), :],
                    send_sem=s2,
                    recv_sem=r2,
                    device_id=(p, j),
                    device_id_type=MESH,
                ).start()

            return 0

        lax.fori_loop(0, ROWS // RL, send_rows, 0)
        return 0

    lax.fori_loop(0, NX * RL, finish, 0)
    for n in range(NX):
        rows[at_row(n), :] = core[lax.rem(i, RL), n, block(i), :]

    for d in range(1, COLS):
        q = col_partner(d)
        pltpu.make_async_remote_copy(
            src_ref=core.at[:, :, pl.ds(pl.multiple_of(q * BL, BL), BL), :],
            dst_ref=core_out.at[pl.ds(j * RL, RL)],
            send_sem=so,
            recv_sem=ro,
            device_id=(i, q),
            device_id_type=MESH,
        ).start()
    own = pltpu.make_async_copy(
        core.at[:, :, pl.ds(pl.multiple_of(j * BL, BL), BL), :],
        core_out.at[pl.ds(j * RL, RL)],
        own_sem.at[0],
    )
    own.start()

    got = rows.at[pl.ds(0, (ROWS - 1) * NX * 8)]
    pltpu.make_async_copy(got, got, r2).wait()
    gh, gl = [], []
    for e in range(8):
        h, l = split(rows[pl.ds(e, ROWS * NX, stride=8), :])
        gh.append(h)
        gl.append(l)
    gh = jnp.concatenate(gh, axis=1)
    gl = jnp.concatenate(gl, axis=1)
    g = dot_t(jnp.concatenate([gh, gl], axis=0), gh)
    cross = g[128:]
    part[...] = (g[:128] + (cross + cross.T)).reshape(16, 8, 128)

    at_xy, at_zk = x * SY + y, z * 2 + k

    def over_xy(d):
        xx, yy = add_mod(x, d // SY, SX), add_mod(y, d % SY, SY)
        return xx * SY + yy, (yy * SZ + z, xx * 2 + k)

    def over_zk(d):
        zz, kk = add_mod(z, d // 2, SZ), add_mod(k, d % 2, 2)
        return (y * SZ + zz, x * 2 + kk)

    for d in XY_ORDER:
        slot, device = over_xy(d)
        pltpu.make_async_remote_copy(
            src_ref=part.at[slot],
            dst_ref=buf_a.at[at_xy],
            send_sem=s3,
            recv_sem=r3,
            device_id=device,
            device_id_type=MESH,
        ).start()
    buf_a[at_xy] = part[at_xy]
    pltpu.make_async_copy(buf_a.at[pl.ds(0, 15)], buf_a.at[pl.ds(0, 15)], r3).wait()

    buf_b[at_zk] = jnp.sum(buf_a[...], axis=0)
    for d in ZK_ORDER:
        pltpu.make_async_remote_copy(
            src_ref=buf_b.at[at_zk],
            dst_ref=buf_b.at[at_zk],
            send_sem=s4,
            recv_sem=r4,
            device_id=over_zk(d),
            device_id_type=MESH,
        ).start()
    pltpu.make_async_copy(buf_b.at[pl.ds(0, 15)], buf_b.at[pl.ds(0, 15)], r4).wait()
    total[...] = jnp.sum(buf_b[...], axis=0) * SCALE

    for d in XY_ORDER:
        pltpu.make_async_remote_copy(
            src_ref=total,
            dst_ref=gram_out.at[at_xy],
            send_sem=s5,
            recv_sem=r5,
            device_id=over_xy(d)[1],
            device_id_type=MESH,
        ).start()
    own_gram = pltpu.make_async_copy(total, gram_out.at[at_xy], own_sem.at[1])
    own_gram.start()

    sent = send_r.at[:, pl.ds(0, R - RL)]
    pltpu.make_async_copy(sent, sent, s1).wait()
    sent = rows.at[pl.ds(0, (ROWS - 1) * NX * 8)]
    pltpu.make_async_copy(sent, sent, s2).wait()
    sent = core.at[:, :, pl.ds(0, B - BL), :]
    pltpu.make_async_copy(sent, sent, so).wait()
    own.wait()
    own_gram.wait()
    for sem in (s3, s4, s5):
        pltpu.make_async_copy(buf_a.at[pl.ds(0, 15)], buf_a.at[pl.ds(0, 15)], sem).wait()
    got = core_out.at[pl.ds(0, R - RL)]
    pltpu.make_async_copy(got, got, ro).wait()
    pltpu.make_async_copy(gram_out.at[pl.ds(0, 15)], gram_out.at[pl.ds(0, 15)], r5).wait()


def place(core, gram, core_out, gram_out, sem):
    copies = [
        pltpu.make_async_copy(core, core_out, sem.at[0]),
        pltpu.make_async_copy(gram, gram_out, sem.at[1]),
    ]
    for c in copies:
        c.start()
    for c in copies:
        c.wait()


def in_vmem(a):
    return pltpu.with_memory_space_constraint(a, pltpu.VMEM)


def in_hbm(a):
    return pltpu.with_memory_space_constraint(a, pltpu.HBM)


def body(tensor, factor_y, factor_z, factor_s):
    dma = pltpu.SemaphoreType.DMA
    core, gram = pl.pallas_call(
        kernel,
        out_shape=(
            jax.ShapeDtypeStruct((R, NX, BL, C), F32),
            jax.ShapeDtypeStruct((16, 8, 128), F32),
        ),
        in_specs=[pl.BlockSpec(memory_space=pltpu.HBM)] * 4,
        out_specs=(pl.BlockSpec(memory_space=pl.ANY), pl.BlockSpec(memory_space=pl.ANY)),
        scratch_shapes=[
            pltpu.VMEM((NY * COLS, B), F32),
            pltpu.VMEM((NZ, C), F32),
            pltpu.VMEM((R, S), F32),
            pltpu.VMEM((NX, S, NY, NZ), F32),
            pltpu.VMEM((NX, R, NY, C), F32),
            pltpu.VMEM((NX, RL, NY * COLS, C), F32),
            pltpu.VMEM((RL, NX, B, C), F32),
            pltpu.VMEM((ROWS * NX * 8, C), F32),
            pltpu.VMEM((16, 8, 128), F32),
            pltpu.VMEM((16, 8, 128), F32),
            pltpu.VMEM((16, 8, 128), F32),
            pltpu.VMEM((8, 128), F32),
            pltpu.VMEM((NZ, 2 * C), BF16),
            pltpu.VMEM((2 * B, NY * COLS), BF16),
            pltpu.VMEM((2 * R * 8, S * 8), BF16),
            pltpu.SemaphoreType.REGULAR,
            dma((3,)),
            dma((NX,)),
            dma, dma((NX, RL)),
            dma, dma,
            dma, dma, dma((2,)),
            dma, dma,
            dma, dma,
            dma, dma,
        ],
        compiler_params=pltpu.CompilerParams(
            collective_id=0, has_side_effects=True, vmem_limit_bytes=VMEM_BYTES
        ),
    )(*(in_hbm(a) for a in (tensor, factor_y, factor_z, factor_s.T)))
    return pl.pallas_call(
        place,
        out_shape=(
            jax.ShapeDtypeStruct((R, NX, BL, C), F32),
            jax.ShapeDtypeStruct((128, 128), F32),
        ),
        in_specs=[pl.BlockSpec(memory_space=pltpu.VMEM)] * 2,
        out_specs=(pl.BlockSpec(memory_space=pl.ANY), pl.BlockSpec(memory_space=pl.ANY)),
        scratch_shapes=[dma((2,))],
        compiler_params=pltpu.CompilerParams(vmem_limit_bytes=2 * 1024 * 1024),
    )(core, gram.reshape(128, 128))


def solution(mesh):
    in_specs = (P(None, "row", "col", None), P(), P(), P())
    out_specs = (P(None, "row", "col", None), P())
    return jax.shard_map(body, mesh=mesh, in_specs=in_specs, out_specs=out_specs, check_vma=False)
```
